256 devices in a mesh: outer: 16 (over y_hi, z), inner: 16 (over y_lo, x, core).
Axes of the slice: x: 4, y: 4 (y_hi: 2, y_lo: 2; y = y_hi * 2 + y_lo), z: 8, core: 2. Of those that a mesh axis runs over, the one named last changes fastest.
Arguments:
- queries: bfloat16 [131072, 1024], P(('outer', 'inner')), may hold values from -4.5 to 4.5
- keys: bfloat16 [131072, 128], P(('outer', 'inner')), may hold values from -4.5 to 4.5
- values: bfloat16 [131072, 128], P(('outer', 'inner')), may hold values from -6 to 6
- key_blocks: int32 [1024, 44], P(('outer', 'inner')), may hold values from 0 to 1023, as said below
- key_counts: int32 [1024], P(('outer', 'inner')), may hold values from 4 to 44, as said below
Outputs:
- context: bfloat16 [131072, 1024], P(('outer', 'inner'))
The draws below stay inside these ranges and needn't reach their ends.
Inputs may be any that keep to these rules, and one draw needn't show every extreme that they name: `key_blocks`: row b lists 44 blocks, the live ones distinct, b itself first; all lie in group b // 64 or in the two groups beside it on the closed cycle of 16 groups; entries from key_counts[b] onward equal b. `key_counts`: some row lists 44 live entries.
All inputs are finite; a program needn't handle non-finite values.
Results may differ from the reference program's by a relative error of at most 0.0047.
Values may be sent and summed in bfloat16 or wider, within the bound.
A program may use at most 128 MiB of HBM per device.

```python
import jax
import jax.numpy as jnp
from jax import lax

HD = 128
HEADS = 8
BLOCK = 128
MAXB = 44
GROUP_BLOCKS = 64
GROUPS = 16
TOKENS = 131072
QBLOCKS = 1024


def pattern(key):
    key = jax.random.fold_in(key, 5)
    first, second, third, fourth = jax.random.split(key, 4)
    cand = 3 * GROUP_BLOCKS
    rows = jnp.arange(QBLOCKS, dtype=jnp.int32)
    spots = jnp.arange(cand, dtype=jnp.int32)
    bits = jax.random.randint(first, (QBLOCKS, cand), 0, 2 ** 20) * 1024 + spots[None, :]
    self_spot = GROUP_BLOCKS + rows % GROUP_BLOCKS
    scored = jnp.where(spots[None, :] == self_spot[:, None], -1, bits)
    chosen = jnp.argsort(scored, axis=1)[:, :MAXB].astype(jnp.int32)
    group_ids = rows // GROUP_BLOCKS
    key_group = (group_ids[:, None] - 1 + chosen // GROUP_BLOCKS + GROUPS) % GROUPS
    listed = key_group * GROUP_BLOCKS + chosen % GROUP_BLOCKS
    lowest = max(4, MAXB // 4)
    spread = MAXB - lowest
    left_factor = jax.random.randint(second, (QBLOCKS,), 0, spread + 1)
    right_factor = jax.random.randint(third, (QBLOCKS,), 0, spread + 1)
    counts = lowest + left_factor * right_factor // max(spread, 1)
    top_row = jax.random.randint(fourth, (), 0, QBLOCKS)
    counts = jnp.where(rows == top_row, MAXB, counts)
    counts = jnp.minimum(counts, MAXB).astype(jnp.int32)
    entries = jnp.arange(MAXB, dtype=jnp.int32)
    listed = jnp.where(entries[None, :] < counts[:, None], listed, rows[:, None]).astype(jnp.int32)
    return (listed, counts)


def draw_queries(key, part):
    key = jax.random.fold_in(key, 11)
    drawn = jnp.clip(jax.random.normal(key, (TOKENS, HEADS * HD)), -4.5, 4.5)
    return drawn.astype(jnp.bfloat16)


def draw_keys(key, part):
    key = jax.random.fold_in(key, 13)
    drawn = jnp.clip(jax.random.normal(key, (TOKENS, HD)), -4.5, 4.5)
    return drawn.astype(jnp.bfloat16)


def draw_key_blocks(key, part):
    base = key
    return pattern(base)[0]


def draw_key_counts(key, part):
    base = key
    return pattern(base)[1]


def block_levels(stream_key, dims, pieces, least, top_value):
    gain = 1.0
    for position, parts in pieces:
        heights = jax.random.uniform(jax.random.fold_in(jax.random.fold_in(stream_key, 6), position), (parts,), jnp.float32, least / len(pieces), top_value / len(pieces))
        gain = gain * jnp.repeat(jnp.exp(heights), dims[position] // parts).reshape((-1,) + (1,) * (len(dims) - 1 - position))
    return gain


def scatter_about(key, extent, scale, reach, cuts=(), held_as=jnp.bfloat16):
    values = scale * jax.random.normal(key, extent, jnp.float32)
    if cuts:
        values = values * block_levels(key, extent, cuts, -0.22, 0.18)
    return jnp.clip(values, -reach, reach).astype(held_as)


def setup_inputs(seed: int = 0) -> dict:
    splits = jax.random.split(jax.random.key(seed), 6)
    queries = draw_queries(jax.random.fold_in(splits[5], 71), 0)
    keys = draw_keys(jax.random.fold_in(splits[5], 71), 0)
    values = scatter_about(splits[2], (TOKENS, HD), 1.0, 6.0, ((0, 256),))
    key_blocks = draw_key_blocks(jax.random.fold_in(splits[5], 71), 0)
    key_counts = draw_key_counts(jax.random.fold_in(splits[5], 71), 0)
    return {"queries": queries, "keys": keys, "values": values, "key_blocks": key_blocks, "key_counts": key_counts}


def reference(queries, keys, values, key_blocks, key_counts):
    key_tiles = keys.reshape(QBLOCKS, BLOCK, HD)
    value_tiles = values.reshape(QBLOCKS, BLOCK, HD)
    query_tiles = queries.reshape(QBLOCKS, BLOCK, HEADS, HD)

    def attend_block(items):
        query_block, block_list, live_count = items
        key_rows = key_tiles[block_list].reshape(MAXB * BLOCK, HD).astype(jnp.float32)
        value_rows = value_tiles[block_list].reshape(MAXB * BLOCK, HD).astype(jnp.float32)
        scores = jnp.einsum('qhd,kd->hqk', query_block.astype(jnp.float32), key_rows) * (HD ** -0.5)
        live_mask = (jnp.arange(MAXB * BLOCK, dtype=jnp.int32) // BLOCK) < live_count
        scores = jnp.where(live_mask[None, None, :], scores, -jnp.inf)
        peak = jnp.max(scores, axis=2, keepdims=True)
        weights = jnp.exp(scores - peak)
        total = jnp.sum(weights, axis=2, keepdims=True)
        rounded = lax.optimization_barrier(weights.astype(jnp.bfloat16)).astype(jnp.float32)
        mixed_rows = jnp.einsum('hqk,kd->hqd', rounded, value_rows) / total
        return jnp.transpose(mixed_rows, (1, 0, 2)).reshape(BLOCK, HEADS * HD).astype(jnp.bfloat16)

    result = lax.map(attend_block, (query_tiles, key_blocks, key_counts))
    return result.reshape(TOKENS, HEADS * HD)
```

```python
import functools

import jax
import jax.numpy as jnp
from jax import lax
from jax.experimental import pallas as pl
from jax.experimental.pallas import tpu as pltpu
from jax.sharding import PartitionSpec as P

HD = 128
HEADS = 8
BLOCK = 128
MAXB = 44
XS = 4
ZS = 8
CH = 4
GROUP_BLOCKS = 64
GROUPS = 16
SCALE = HD ** -0.5 * 1.4426950408889634
LIMIT = 2.0 ** 100
STEP = 2
MESH = pl.DeviceIdType.MESH

LINKS = ("xp", "xm", "y", "zp", "zm")
STEPS = (
    {"xp": (1, 0, 0), "xm": (3, 0, 0), "y": (0, 1, 0), "zp": (0, 0, 1), "zm": (0, 0, -1)},
    {"xp": (2, 0, 0), "xm": (3, 1, 0), "y": (1, 1, 0), "zp": (1, 0, 1), "zm": (3, 0, -1)},
    {"xp": (2, 0, 1), "xm": (2, 0, -1), "y": (2, 1, 0), "zp": (0, 1, 1), "zm": (0, 1, -1)},
    {"xp": (1, 1, 1), "xm": (3, 1, -1), "y": (2, 1, 1), "zp": (3, 0, 1), "zm": (1, 0, -1)},
)
LAST = (
    (("xp", (1, 1, -1), 0), ("xm", (3, 1, 1), 0), ("y", (2, 1, -1), 0), ("zp", (3, 1, 1), 2), ("zm", (1, 1, -1), 2)),
    (("xp", (1, 1, -1), 1), ("xm", (3, 1, 1), 1), ("y", (2, 1, -1), 1), ("zp", (3, 1, 1), 3), ("zm", (1, 1, -1), 3)),
    (("xm", (2, 1, -1), 2), ("y", (2, 1, -1), 3)),
)


def gather_kernel(k_ref, v_ref, win, own_sem, send_sem, recv_sem, sib_send, sib_recv):
    g = lax.axis_index("outer")
    inner = lax.axis_index("inner")
    core = inner % 2
    x = inner // 2 % XS
    y = inner // (2 * XS)
    cross_up = jnp.where(g % ZS == ZS - 1, 1, 0)
    cross_down = jnp.where(g % ZS == 0, 1, 0)
    up, down = (g + 1) % GROUPS, (g + GROUPS - 1) % GROUPS

    def place(px, py):
        return (py * XS + px) * 2 + core

    target = {
        "xp": (g, place((x + XS - 1) % XS, y)),
        "xm": (g, place((x + 1) % XS, y)),
        "y": (g, place(x, 1 - y)),
        "zp": (down, place(x, (y + cross_down) % 2)),
        "zm": (up, place(x, (y + cross_up) % 2)),
    }
    sibling = (g, (y * XS + x) * 2 + 1 - core)

    def slot(piece):
        dx, dy, dz = piece
        turn = {0: 0, 1: cross_up, -1: cross_down}[dz]
        return dz + 1, place((x + dx) % XS, (y + dy + turn) % 2)

    def sent(link, piece):
        dx, dy, dz = piece
        by = {
            "xp": ((dx + XS - 1) % XS, dy, dz),
            "xm": ((dx + 1) % XS, dy, dz),
            "y": (dx, 1 - dy, dz),
            "zp": (dx, dy, dz - 1),
            "zm": (dx, dy, dz + 1),
        }[link]
        return by, dz + 1

    def link_copy(link, piece, c, step):
        n = LINKS.index(link)
        mine, there = sent(link, piece)
        a, b = slot(mine)
        return pltpu.make_async_remote_copy(
            src_ref=win.at[a, b, c],
            dst_ref=win.at[there, b, c],
            send_sem=send_sem.at[n, step, c],
            recv_sem=recv_sem.at[n, step, c],
            device_id=target[link],
            device_id_type=MESH,
        )

    def arrival(link, piece, c, step):
        n = LINKS.index(link)
        a, b = slot(piece)
        return pltpu.make_async_remote_copy(
            src_ref=win.at[a, b, c],
            dst_ref=win.at[a, b, c],
            send_sem=send_sem.at[n, step, c],
            recv_sem=recv_sem.at[n, step, c],
            device_id=target[link],
            device_id_type=MESH,
        )

    def sib_copy(piece, c, n, step):
        a, b = slot(piece)
        return pltpu.make_async_remote_copy(
            src_ref=win.at[a, b, c],
            dst_ref=win.at[a, b, c],
            send_sem=sib_send.at[n, step, c],
            recv_sem=sib_recv.at[n, step, c],
            device_id=sibling,
            device_id_type=MESH,
        )

    def sib_arrival(piece, c, n, step):
        a, b = slot(piece)
        return pltpu.make_async_remote_copy(
            src_ref=win.at[a, b, c],
            dst_ref=win.at[a, b + 1 - 2 * core, c],
            send_sem=sib_send.at[n, step, c],
            recv_sem=sib_recv.at[n, step, c],
            device_id=sibling,
            device_id_type=MESH,
        )

    own = (0, 0, 0)
    _, here = slot(own)
    fill = []
    for c in range(CH):
        rows = pl.ds(c * BLOCK, BLOCK)
        for part, ref in enumerate((k_ref, v_ref)):
            copy = pltpu.make_async_copy(ref.at[rows], win.at[1, here, c, part], own_sem.at[c, part])
            copy.start()
            fill.append(copy)

    barrier = pltpu.get_barrier_semaphore()
    for device in (*target.values(), sibling):
        pl.semaphore_signal(barrier, inc=1, device_id=device, device_id_type=MESH)
    pl.semaphore_wait(barrier, len(target) + 1)

    def tick(step, c):
        if step > 0:
            for n, link in enumerate(LINKS):
                piece = STEPS[step - 1][link]
                arrival(link, piece, c, step - 1).wait_recv()
        for n, link in enumerate(LINKS):
            link_copy(link, STEPS[step][link], c, step).start()
        if step > 0:
            for n, link in enumerate(LINKS):
                sib_copy(STEPS[step - 1][link], c, n, step - 1).start()
        else:
            sib_copy(own, c, len(LINKS), 0).start()

    for c in range(CH):
        fill[2 * c].wait()
        fill[2 * c + 1].wait()
        tick(0, c)
    for step in range(1, len(STEPS)):
        lax.fori_loop(0, CH, lambda c, _, step=step: (tick(step, c), 0)[1], 0)

    last = len(STEPS)
    for i in range(CH):
        for n, link in enumerate(LINKS):
            arrival(link, STEPS[last - 1][link], i, last - 1).wait_recv()
        if i < len(LAST):
            for link, piece, c in LAST[i]:
                link_copy(link, piece, c, last).start()
        for n, link in enumerate(LINKS):
            sib_copy(STEPS[last - 1][link], i, n, last - 1).start()
    for row in LAST:
        for link, piece, c in row:
            arrival(link, piece, c, last).wait_recv()
            sib_copy(piece, c, LINKS.index(link), last).start()

    def drain(c, _):
        for step in range(len(STEPS)):
            for n, link in enumerate(LINKS):
                piece = STEPS[step][link]
                link_copy(link, piece, c, step).wait_send()
                sib_copy(piece, c, n, step).wait_send()
                sib_arrival(piece, c, n, step).wait_recv()
        sib_copy(own, c, len(LINKS), 0).wait_send()
        sib_arrival(own, c, len(LINKS), 0).wait_recv()
        return 0

    lax.fori_loop(0, CH, drain, 0)
    for row in LAST:
        for link, piece, c in row:
            n = LINKS.index(link)
            link_copy(link, piece, c, last).wait_send()
            sib_copy(piece, c, n, last).wait_send()
            sib_arrival(piece, c, n, last).wait_recv()


def gather(keys, values):
    steps = len(STEPS) + 1
    return pl.pallas_call(
        gather_kernel,
        out_shape=jax.ShapeDtypeStruct((3, GROUP_BLOCKS // CH, CH, 2, BLOCK, HD), jnp.bfloat16),
        in_specs=[pl.BlockSpec(memory_space=pl.ANY)] * 2,
        out_specs=pl.BlockSpec(memory_space=pl.ANY),
        scratch_shapes=[
            pltpu.SemaphoreType.DMA((CH, 2)),
            pltpu.SemaphoreType.DMA((len(LINKS), steps, CH)),
            pltpu.SemaphoreType.DMA((len(LINKS), steps, CH)),
            pltpu.SemaphoreType.DMA((len(LINKS) + 1, steps, CH)),
            pltpu.SemaphoreType.DMA((len(LINKS) + 1, steps, CH)),
        ],
        compiler_params=pltpu.CompilerParams(collective_id=0, has_side_effects=True),
    )(keys, values)


def nt_dot(a, b):
    return lax.dot_general(a, b, (((1,), (1,)), ((), ())), preferred_element_type=jnp.float32)


def attend_kernel(blocks, counts, q_ref, win, o_ref, kv, shift, acc, sem):
    i = pl.program_id(0)
    g = lax.axis_index("outer")
    half = i % 2

    def fetch(row, side, e):
        block = blocks[row, e]
        group = (block // GROUP_BLOCKS - g + 1 + GROUPS) % GROUPS
        return pltpu.make_async_copy(
            win.at[group * GROUP_BLOCKS + block % GROUP_BLOCKS], kv.at[side, e], sem.at[side, e]
        )

    def entries(row):
        return (counts[row] + STEP - 1) // STEP * STEP

    def fetch_row(row, side):
        lax.fori_loop(0, entries(row), lambda e, _: (fetch(row, side, e).start(), 0)[1], 0)

    @pl.when(i == 0)
    def _():
        fetch_row(0, 0)

    @pl.when(i + 1 < pl.num_programs(0))
    def _():
        fetch_row(i + 1, 1 - half)

    count = counts[i]
    queries = [q_ref[:, h * HD:(h + 1) * HD] for h in range(HEADS)]
    acc[...] = jnp.zeros_like(acc)

    def attend(s, _):
        first = s * STEP
        for e in range(STEP):
            fetch(i, half, first + e).wait()

        @pl.when(s == 0)
        def _():
            k = kv[half, 0, 0]
            for h in range(HEADS):
                peak = jnp.max(nt_dot(q_ref[:, h * HD:(h + 1) * HD], k), axis=1, keepdims=True)
                shift[h] = jnp.broadcast_to(peak * SCALE, (BLOCK, HD))

        k = jnp.concatenate([kv[half, first + e, 0] for e in range(STEP)], axis=0)
        v = []
        for e in range(STEP):
            live = jnp.where(first + e < count, 1.0, 0.0).astype(jnp.float32)
            ones = jnp.full((BLOCK, HD), live, jnp.float32).astype(jnp.bfloat16)
            v.append(jnp.concatenate([kv[half, first + e, 1] * ones, ones], axis=1))
        v = jnp.concatenate(v, axis=0)
        for h in range(HEADS):
            scores = nt_dot(q_ref[:, h * HD:(h + 1) * HD], k)
            m = jnp.concatenate([shift[h]] * STEP, axis=1)
            weights = jnp.exp2(scores * SCALE - m).astype(jnp.bfloat16)
            acc[h] += jnp.dot(weights, v, preferred_element_type=jnp.float32)
        return 0

    lax.fori_loop(0, entries(i) // STEP, attend, 0)
    top = jnp.max(acc[:, :, HD:])
    safe = top < LIMIT

    @pl.when(jnp.logical_not(safe))
    def _():
        def head(h, _):
            q = jnp.zeros((BLOCK, HD), jnp.bfloat16)
            for n in range(HEADS):
                q = jnp.where(h == n, queries[n], q)

            def one(e, state):
                peak, total, mixed = state
                scores = nt_dot(q, kv[half, e, 0]) * SCALE
                new = jnp.maximum(peak, jnp.max(scores, axis=1, keepdims=True))
                weights = jnp.exp2(scores - new)
                keep = jnp.exp2(peak - new)
                total = total * keep + jnp.sum(weights, axis=1, keepdims=True)
                mixed = mixed * keep + jnp.dot(
                    weights.astype(jnp.bfloat16), kv[half, e, 1], preferred_element_type=jnp.float32
                )
                return new, total, mixed

            start = (
                jnp.full((BLOCK, 1), -1e30, jnp.float32),
                jnp.zeros((BLOCK, 1), jnp.float32),
                jnp.zeros((BLOCK, HD), jnp.float32),
            )
            _, total, mixed = lax.fori_loop(0, count, one, start)
            acc[h] = jnp.concatenate([mixed, jnp.broadcast_to(total, (BLOCK, HD))], axis=1)
            return 0

        lax.fori_loop(0, HEADS, head, 0)

    for h in range(HEADS):
        o_ref[:, h * HD:(h + 1) * HD] = (acc[h, :, :HD] / acc[h, :, HD:]).astype(jnp.bfloat16)


def attend(blocks, counts, queries, window):
    rows = queries.shape[0] // BLOCK
    return pl.pallas_call(
        attend_kernel,
        grid_spec=pltpu.PrefetchScalarGridSpec(
            num_scalar_prefetch=2,
            grid=(rows,),
            in_specs=[
                pl.BlockSpec((BLOCK, HEADS * HD), lambda i, *_: (i, 0)),
                pl.BlockSpec(memory_space=pl.ANY),
            ],
            out_specs=pl.BlockSpec((BLOCK, HEADS * HD), lambda i, *_: (i, 0)),
            scratch_shapes=[
                pltpu.VMEM((2, MAXB, 2, BLOCK, HD), jnp.bfloat16),
                pltpu.VMEM((HEADS, BLOCK, HD), jnp.float32),
                pltpu.VMEM((HEADS, BLOCK, 2 * HD), jnp.float32),
                pltpu.SemaphoreType.DMA((2, MAXB)),
            ],
        ),
        out_shape=jax.ShapeDtypeStruct(queries.shape, jnp.bfloat16),
        compiler_params=pltpu.CompilerParams(vmem_limit_bytes=32 * 2 ** 20),
    )(blocks, counts, queries, window)


def body(queries, keys, values, key_blocks, key_counts):
    window = gather(keys, values)
    window = window.reshape(3 * GROUP_BLOCKS, 2, BLOCK, HD)
    return attend(key_blocks, key_counts, queries, window)


def solution(mesh):
    placed = (
        P(("outer", "inner"), None),
        P(("outer", "inner"), None),
        P(("outer", "inner"), None),
        P(("outer", "inner"), None),
        P(("outer", "inner")),
    )
    return jax.shard_map(
        body, mesh=mesh, in_specs=placed, out_specs=P(("outer", "inner"), None), check_vma=False
    )
```

```python
import functools

import jax
import jax.numpy as jnp
from jax import lax
from jax.experimental import pallas as pl
from jax.experimental.pallas import tpu as pltpu
from jax.sharding import PartitionSpec as P

HD = 128
HEADS = 8
BLOCK = 128
MAXB = 44
XS = 4
ZS = 8
CH = 4
GROUP_BLOCKS = 64
STEP = 4
TILE = 2 * HD
GROUPS = 16
SCALE = HD ** -0.5 * 1.4426950408889634
LIMIT = 2.0 ** 100
DEAD = 1e30
MESH = pl.DeviceIdType.MESH

LINKS = ("xp", "xm", "y", "zp", "zm")
STEPS = (
    {"xp": (1, 0, 0), "xm": (3, 0, 0), "y": (0, 1, 0), "zp": (0, 0, 1), "zm": (0, 0, -1)},
    {"xp": (2, 0, 0), "xm": (3, 0, 1), "y": (1, 1, 0), "zp": (1, 0, 1), "zm": (3, 0, -1)},
    {"xp": (1, 0, -1), "xm": (3, 1, 0), "y": (2, 1, 0), "zp": (0, 1, 1), "zm": (0, 1, -1)},
    {"xp": (2, 0, 1), "xm": (2, 0, -1), "y": (3, 1, 1), "zp": (1, 1, 1), "zm": (1, 1, -1)},
)
LAST = (
    (("xm", (3, 1, -1), 0), ("y", (3, 1, -1), 2), ("zp", (2, 1, 1), 1), ("zm", (2, 1, -1), 1)),
    (("xp", (2, 1, 1), 0), ("xm", (3, 1, -1), 1), ("y", (3, 1, -1), 3), ("zp", (2, 1, 1), 2), ("zm", (2, 1, -1), 2)),
    (("y", (2, 1, -1), 0), ("zp", (2, 1, 1), 3), ("zm", (2, 1, -1), 3)),
)
ORDER = ((0, 0, 0),) + tuple(row[link] for row in STEPS for link in LINKS) + ((3, 1, -1), (2, 1, 1), (2, 1, -1))
TICKS = CH * len(STEPS) + len(LAST)
AHEAD = 4


def parent(link, piece):
    dx, dy, dz = piece
    return {
        "xp": ((dx + XS - 1) % XS, dy, dz),
        "xm": ((dx + 1) % XS, dy, dz),
        "y": (dx, 1 - dy, dz),
        "zp": (dx, dy, dz - 1),
        "zm": (dx, dy, dz + 1),
    }[link]


def position():
    g = lax.axis_index("outer")
    inner = lax.axis_index("inner")
    cross_up = jnp.where(g % ZS == ZS - 1, 1, 0)
    cross_down = jnp.where(g % ZS == 0, 1, 0)
    return g, inner // (2 * XS), inner // 2 % XS, inner % 2, cross_up, cross_down


def gather_kernel(k_ref, v_ref, win, stage, own_sem, send_sem, recv_sem, sib_send, sib_recv):
    g, y, x, core, cross_up, cross_down = position()
    up, down = (g + 1) % GROUPS, (g + GROUPS - 1) % GROUPS

    def place(px, py):
        return (py * XS + px) * 2 + core

    target = {
        "xp": (g, place((x + XS - 1) % XS, y)),
        "xm": (g, place((x + 1) % XS, y)),
        "y": (g, place(x, 1 - y)),
        "zp": (down, place(x, (y + cross_down) % 2)),
        "zm": (up, place(x, (y + cross_up) % 2)),
    }
    sibling = (g, (y * XS + x) * 2 + 1 - core)

    def at(piece, c):
        return win.at[ORDER.index(piece), core, c]

    def source(piece, c):
        return stage.at[c] if piece == ORDER[0] else at(piece, c)

    def link_copy(link, piece, c, t):
        n = LINKS.index(link)
        return pltpu.make_async_remote_copy(
            src_ref=source(parent(link, piece), c),
            dst_ref=at(piece, c),
            send_sem=send_sem.at[n, t],
            recv_sem=recv_sem.at[n, t],
            device_id=target[link],
            device_id_type=MESH,
        )

    def sib_copy(piece, c, n, t):
        return pltpu.make_async_remote_copy(
            src_ref=source(piece, c),
            dst_ref=at(piece, c),
            send_sem=sib_send.at[n, t],
            recv_sem=sib_recv.at[n, t],
            device_id=sibling,
            device_id_type=MESH,
        )

    def sib_arrival(piece, c, n, t):
        here = win.at[ORDER.index(piece), 1 - core, c]
        return pltpu.make_async_remote_copy(
            src_ref=here,
            dst_ref=here,
            send_sem=sib_send.at[n, t],
            recv_sem=sib_recv.at[n, t],
            device_id=sibling,
            device_id_type=MESH,
        )

    barrier = pltpu.get_barrier_semaphore()
    for device in (*target.values(), sibling):
        pl.semaphore_signal(barrier, inc=1, device_id=device, device_id_type=MESH)
    fill = []
    for c in range(CH):
        rows = pl.ds(c * BLOCK, BLOCK)
        stage[c, 0] = k_ref[rows]
        stage[c, 1] = v_ref[rows].T
        copy = pltpu.make_async_copy(stage.at[c], at(ORDER[0], c), own_sem.at[c])
        copy.start()
        fill.append(copy)
    pl.semaphore_wait(barrier, len(target) + 1)

    def row(step, c):
        if step < len(STEPS):
            return [(link, STEPS[step][link], c) for link in LINKS]
        return LAST[c]

    def tick(step, c):
        t = step * CH + c
        if isinstance(t, int) and t < CH:
            arrived = ()
        else:
            arrived = row(step - 1, c)
        for link, piece, chunk in arrived:
            link_copy(link, piece, chunk, t - CH).wait_recv()
        for link, piece, chunk in row(step, c) if not (step == len(STEPS) and c >= len(LAST)) else ():
            if not (isinstance(t, int) and t < AHEAD):
                link_copy(link, piece, chunk, t - AHEAD).wait_send()
            link_copy(link, piece, chunk, t).start()
        for link, piece, chunk in arrived:
            sib_copy(piece, chunk, LINKS.index(link), t - CH).start()
        if step == 0:
            sib_copy(ORDER[0], c, len(LINKS), t).start()

    for c in range(CH):
        tick(0, c)
    for step in range(1, len(STEPS)):
        lax.fori_loop(0, CH, lambda c, _, step=step: (tick(step, c), 0)[1], 0)
    for c in range(CH):
        tick(len(STEPS), c)
    for c, last in enumerate(LAST):
        t = TICKS - len(LAST) + c
        for link, piece, chunk in last:
            link_copy(link, piece, chunk, t).wait_recv()
            sib_copy(piece, chunk, LINKS.index(link), t).start()

    sent = {link: [] for link in LINKS}
    for t in range(TICKS):
        for link, piece, chunk in row(t // CH, t % CH):
            if t >= AHEAD:
                sent[link].remove(t - AHEAD)
            sent[link].append(t)
    for link in LINKS:
        for t in sent[link]:
            link_copy(link, ORDER[1], 0, t).wait_send()
    for copy in fill:
        copy.wait()

    def drain(c, _):
        for step in range(len(STEPS)):
            for link, piece, chunk in row(step, c):
                sib_copy(piece, chunk, LINKS.index(link), step * CH + c).wait_send()
                sib_arrival(piece, chunk, LINKS.index(link), step * CH + c).wait_recv()
        sib_copy(ORDER[0], c, len(LINKS), c).wait_send()
        sib_arrival(ORDER[0], c, len(LINKS), c).wait_recv()
        return 0

    lax.fori_loop(0, CH, drain, 0)
    for c, last in enumerate(LAST):
        for link, piece, chunk in last:
            t = TICKS - len(LAST) + c
            sib_copy(piece, chunk, LINKS.index(link), t).wait_send()
            sib_arrival(piece, chunk, LINKS.index(link), t).wait_recv()


def gather(keys, values):
    return pl.pallas_call(
        gather_kernel,
        out_shape=jax.ShapeDtypeStruct((len(ORDER), 2, CH, 2, BLOCK, HD), jnp.bfloat16),
        in_specs=[pl.BlockSpec(memory_space=pltpu.VMEM)] * 2,
        out_specs=pl.BlockSpec(memory_space=pl.ANY),
        scratch_shapes=[
            pltpu.VMEM((CH, 2, BLOCK, HD), jnp.bfloat16),
            pltpu.SemaphoreType.DMA((CH,)),
            pltpu.SemaphoreType.DMA((len(LINKS), TICKS)),
            pltpu.SemaphoreType.DMA((len(LINKS), TICKS)),
            pltpu.SemaphoreType.DMA((len(LINKS) + 1, TICKS)),
            pltpu.SemaphoreType.DMA((len(LINKS) + 1, TICKS)),
        ],
        compiler_params=pltpu.CompilerParams(collective_id=0, has_side_effects=True),
    )(keys, values)


def nt_dot(a, b):
    return lax.dot_general(a, b, (((1,), (1,)), ((), ())), preferred_element_type=jnp.float32)


def query_tile(q_ref, row, t):
    rows = pl.ds(pl.multiple_of(row * BLOCK, BLOCK), BLOCK)
    return jnp.concatenate([q_ref[rows, h * HD:(h + 1) * HD] for h in (2 * t, 2 * t + 1)], axis=0)


def attend_kernel(
    blocks, counts, q_ref, k_ref, win, o_ref, kv, scores, shift, total, acc, places, rows_of, live, first_of, sem
):
    g, y, x, _, cross_up, cross_down = position()
    lists = q_ref.shape[0] // BLOCK
    tiles = [pl.ds(t * TILE, TILE) for t in range(HEADS * HD // TILE)]

    for i, (dx, dy, dz) in enumerate(ORDER):
        places[(dz + 1) * 2 * XS + dy * XS + dx] = i

    def rank(block):
        group = (block // GROUP_BLOCKS - g + 1 + GROUPS) % GROUPS
        device = block % GROUP_BLOCKS // CH
        turn = jnp.where(group == 2, cross_up, jnp.where(group == 0, cross_down, 0))
        dx = (device // 2 % XS - x + XS) % XS
        dy = (device // (2 * XS) + y + turn) % 2
        return (places[group * 2 * XS + dy * XS + dx] * 2 + device % 2) * CH + block % CH

    def fetch(n, e, source):
        return pltpu.make_async_copy(win.at[source], kv.at[n, e], sem.at[n, e])

    def plan(row, n):
        count = counts[row]
        first_of[row] = n

        def one(s, n):
            rows_of[n] = row
            for e in range(STEP):
                live[n, e] = (s * STEP + e < count).astype(jnp.int32)
                fetch(n, e, rank(blocks[row, s * STEP + e])).start()
            return n + 1

        return lax.fori_loop(0, (count + STEP - 1) // STEP, one, n)

    steps = lax.fori_loop(0, lists, plan, 0)

    def wait(n):
        for e in range(STEP):
            fetch(n, e, 0).wait()

    total[...] = jnp.zeros_like(total)
    acc[...] = jnp.zeros_like(acc)

    def peaks(row, _):
        own = k_ref[pl.ds(pl.multiple_of(row * BLOCK, BLOCK), BLOCK)]
        for t, c in enumerate(tiles):
            s = nt_dot(own, query_tile(q_ref, row, t))
            shift[row, :, c] = jnp.broadcast_to(jnp.max(s, axis=0, keepdims=True) * SCALE, (8, TILE))
        return 0

    lax.fori_loop(0, lists, peaks, 0)

    def keys_of(n):
        return jnp.concatenate([kv[n, e, 0] for e in range(STEP)], axis=0)

    wait(0)
    for t, c in enumerate(tiles):
        scores[:, c] = nt_dot(keys_of(0), query_tile(q_ref, 0, t))

    def step(n, _):
        row = rows_of[n]
        following = jnp.minimum(n + 1, steps - 1)

        @pl.when(n + 1 < steps)
        def _():
            wait(n + 1)

        next_row = rows_of[following]
        k = keys_of(following)
        v = jnp.concatenate([kv[n, e, 1] for e in range(STEP)], axis=1)
        for t, c in enumerate(tiles):
            base = shift[row, 0:1, c]
            parts = []
            for e in range(STEP):
                m = jnp.where(live[n, e] == 1, base, DEAD)
                parts.append(jnp.exp2(scores[pl.ds(e * BLOCK, BLOCK), c] * SCALE - m))
            scores[:, c] = nt_dot(k, query_tile(q_ref, next_row, t))
            weights = jnp.concatenate(parts, axis=0)
            total[row, :, c] += jnp.sum(weights.reshape(STEP * BLOCK // 8, 8, TILE), axis=0)
            acc[row, :, c] += jnp.dot(v, weights.astype(jnp.bfloat16), preferred_element_type=jnp.float32)
        return 0

    lax.fori_loop(0, steps, step, 0)

    def finish(row, _):
        sums = jnp.sum(total[row], axis=0, keepdims=True)
        safe = jnp.max(sums) < LIMIT

        @pl.when(jnp.logical_not(safe))
        def _():
            for t, c in enumerate(tiles):
                q = query_tile(q_ref, row, t)

                def one(e, state, q=q):
                    peak, tot, mixed = state
                    n = first_of[row] + e // STEP
                    s = nt_dot(kv[n, e % STEP, 0], q) * SCALE
                    new = jnp.maximum(peak, jnp.max(s, axis=0, keepdims=True))
                    weights = jnp.exp2(s - new)
                    keep = jnp.exp2(peak - new)
                    tot = tot * keep + jnp.sum(weights, axis=0, keepdims=True)
                    mixed = mixed * keep + jnp.dot(
                        kv[n, e % STEP, 1], weights.astype(jnp.bfloat16), preferred_element_type=jnp.float32
                    )
                    return new, tot, mixed

                start = (
                    jnp.full((1, TILE), -DEAD, jnp.float32),
                    jnp.zeros((1, TILE), jnp.float32),
                    jnp.zeros((HD, TILE), jnp.float32),
                )
                _, tot, mixed = lax.fori_loop(0, counts[row], one, start)
                total[row, :, c] = jnp.concatenate([tot, jnp.zeros((7, TILE), jnp.float32)], axis=0)
                acc[row, :, c] = mixed

        sums = jnp.sum(total[row], axis=0, keepdims=True)
        rows = pl.ds(pl.multiple_of(row * BLOCK, BLOCK), BLOCK)
        for h in range(HEADS):
            c = slice(h * HD, (h + 1) * HD)
            o_ref[rows, c] = (acc[row, :, c] / sums[:, c]).T.astype(jnp.bfloat16)
        return 0

    lax.fori_loop(0, lists, finish, 0)


def attend(blocks, counts, queries, keys, window):
    lists = queries.shape[0] // BLOCK
    steps = lists * (MAXB // STEP)
    rows = HEADS * BLOCK
    return pl.pallas_call(
        attend_kernel,
        in_specs=[pl.BlockSpec(memory_space=pltpu.SMEM)] * 2
        + [pl.BlockSpec(memory_space=pltpu.VMEM)] * 2
        + [pl.BlockSpec(memory_space=pl.ANY)],
        out_specs=pl.BlockSpec(memory_space=pltpu.VMEM),
        scratch_shapes=[
            pltpu.VMEM((steps, STEP, 2, BLOCK, HD), jnp.bfloat16),
            pltpu.VMEM((STEP * BLOCK, rows), jnp.float32),
            pltpu.VMEM((lists, 8, rows), jnp.float32),
            pltpu.VMEM((lists, 8, rows), jnp.float32),
            pltpu.VMEM((lists, HD, rows), jnp.float32),
            pltpu.SMEM((len(ORDER),), jnp.int32),
            pltpu.SMEM((steps,), jnp.int32),
            pltpu.SMEM((steps, STEP), jnp.int32),
            pltpu.SMEM((lists,), jnp.int32),
            pltpu.SemaphoreType.DMA((steps, STEP)),
        ],
        out_shape=jax.ShapeDtypeStruct(queries.shape, jnp.bfloat16),
        compiler_params=pltpu.CompilerParams(vmem_limit_bytes=40 * 2 ** 20),
    )(blocks, counts, queries, keys, window)


def body(queries, keys, values, key_blocks, key_counts):
    window = gather(keys, values)
    window = window.reshape(len(ORDER) * 2 * CH, 2, BLOCK, HD)
    return attend(key_blocks, key_counts, queries, keys, window)


def solution(mesh):
    placed = (
        P(("outer", "inner"), None),
        P(("outer", "inner"), None),
        P(("outer", "inner"), None),
        P(("outer", "inner"), None),
        P(("outer", "inner")),
    )
    return jax.shard_map(
        body, mesh=mesh, in_specs=placed, out_specs=P(("outer", "inner"), None), check_vma=False
    )
```

```python
import functools

import jax
import jax.numpy as jnp
from jax import lax
from jax.experimental import pallas as pl
from jax.experimental.pallas import tpu as pltpu
from jax.sharding import PartitionSpec as P

HD = 128
HEADS = 8
BLOCK = 128
MAXB = 44
XS = 4
ZS = 8
CH = 4
GROUP_BLOCKS = 64
STEP = 4
TILE = 2 * HD
GROUPS = 16
SCALE = HD ** -0.5 * 1.4426950408889634
LIMIT = 2.0 ** 100
DEAD = 1e30
LANES = 128
VMEM_LIMIT = 60 * 2 ** 20
MESH = pl.DeviceIdType.MESH

LINKS = ("xp", "xm", "y", "zp", "zm")
STEPS = (
    {"xp": (1, 0, 0), "xm": (3, 0, 0), "y": (0, 1, 0), "zp": (0, 0, 1), "zm": (0, 0, -1)},
    {"xp": (2, 0, 0), "xm": (3, 0, 1), "y": (1, 1, 0), "zp": (1, 0, 1), "zm": (3, 0, -1)},
    {"xp": (1, 0, -1), "xm": (3, 1, 0), "y": (2, 1, 0), "zp": (0, 1, 1), "zm": (0, 1, -1)},
    {"xp": (2, 0, 1), "xm": (2, 0, -1), "y": (3, 1, 1), "zp": (1, 1, 1), "zm": (1, 1, -1)},
)
LAST = (
    (("xm", (3, 1, -1), 0), ("y", (3, 1, -1), 2), ("zp", (2, 1, 1), 1), ("zm", (2, 1, -1), 1)),
    (("xp", (2, 1, 1), 0), ("xm", (3, 1, -1), 1), ("y", (3, 1, -1), 3), ("zp", (2, 1, 1), 2), ("zm", (2, 1, -1), 2)),
    (("y", (2, 1, -1), 0), ("zp", (2, 1, 1), 3), ("zm", (2, 1, -1), 3)),
)
ORDER = ((0, 0, 0),) + tuple(row[link] for row in STEPS for link in LINKS) + ((3, 1, -1), (2, 1, 1), (2, 1, -1))
STAGES = ((0, 11, 12), (11, 16, 8), (16, 21, 8))
TICKS = CH * len(STEPS) + len(LAST)
AHEAD = 4


def parent(link, piece):
    dx, dy, dz = piece
    return {
        "xp": ((dx + XS - 1) % XS, dy, dz),
        "xm": ((dx + 1) % XS, dy, dz),
        "y": (dx, 1 - dy, dz),
        "zp": (dx, dy, dz - 1),
        "zm": (dx, dy, dz + 1),
    }[link]


def position():
    g = lax.axis_index("outer")
    inner = lax.axis_index("inner")
    cross_up = jnp.where(g % ZS == ZS - 1, 1, 0)
    cross_down = jnp.where(g % ZS == 0, 1, 0)
    return g, inner // (2 * XS), inner // 2 % XS, inner % 2, cross_up, cross_down


def nt_dot(a, b):
    return lax.dot_general(a, b, (((1,), (1,)), ((), ())), preferred_element_type=jnp.float32)


def query_tile(q_ref, row, t):
    rows = pl.ds(pl.multiple_of(row * BLOCK, BLOCK), BLOCK)
    return jnp.concatenate([q_ref[rows, h * HD:(h + 1) * HD] for h in (2 * t, 2 * t + 1)], axis=0)


def tiles():
    return [(t, pl.ds(t * TILE, TILE)) for t in range(HEADS * HD // TILE)]


def ahead(k_ref, q_ref, row, scores):
    for t, c in tiles():
        scores[:, c] = nt_dot(k_ref, query_tile(q_ref, row, t))


def attend_step(q_ref, scores, shift, total, acc, row, live, v, next_row, next_k):
    for t, c in tiles():
        base = shift[row, 0:1, c]
        parts = []
        for e in range(STEP):
            m = jnp.where(live[e], base, DEAD)
            parts.append(jnp.exp2(scores[pl.ds(e * BLOCK, BLOCK), c] * SCALE - m))
        scores[:, c] = nt_dot(next_k, query_tile(q_ref, next_row, t))
        weights = jnp.concatenate(parts, axis=0)
        total[row, :, c] += jnp.sum(weights.reshape(STEP * BLOCK // 8, 8, TILE), axis=0)
        acc[row, :, c] += jnp.dot(v, weights.astype(jnp.bfloat16), preferred_element_type=jnp.float32)


def sort_lists(blocks, counts, lists, pad, flat, table):
    g, y, x, _, cross_up, cross_down = position()
    pad[...] = jnp.zeros_like(pad)
    pad[0:lists, 0:MAXB] = blocks[...]
    block = pad[...]
    lane = lax.broadcasted_iota(jnp.int32, (8, LANES), 1)
    line = lax.broadcasted_iota(jnp.int32, (8, LANES), 0)
    length = jnp.zeros((8, LANES), jnp.int32)
    for row in range(lists):
        length = jnp.where(line == row, counts[row], length)
    group = (block // GROUP_BLOCKS - g + 1 + GROUPS) % GROUPS
    device = block % GROUP_BLOCKS // CH
    turn = jnp.where(group == 2, cross_up, jnp.where(group == 0, cross_down, 0))
    dx = (device // 2 % XS - x + XS) % XS
    dy = (device // (2 * XS) + y + turn) % 2
    code = group * 2 * XS + dy * XS + dx
    order = jnp.zeros_like(code)
    for i, (px, py, pz) in enumerate(ORDER):
        order = jnp.where(code == (pz + 1) * 2 * XS + py * XS + px, i, order)
    rank = (order * 2 + device % 2) * CH + block % CH

    def before(mask):
        ones = jnp.where(mask, 1, 0)
        count = ones
        for k in (1, 2, 4, 8, 16, 32):
            count = count + jnp.where(lane >= k, pltpu.roll(count, k, 1), 0)
        return count - ones

    rest = lane < length
    key = jnp.full((8, LANES), -1, jnp.int32)
    for kind, (first, end, slots) in enumerate(STAGES):
        mask = (lane < length) & (order >= first) & (order < end)
        place = before(mask)
        mask = mask & (place < slots)
        key = jnp.where(mask, kind * LANES + place, key)
        rest = rest & jnp.logical_not(mask)
    key = jnp.where(rest, len(STAGES) * LANES + before(rest), key)
    flat[...] = jnp.full((LANES, LANES), -1, jnp.int32)
    flat[0:8] = key
    keys = flat[...].T
    flat[0:8] = rank
    ranks = flat[...].T
    lane = lax.broadcasted_iota(jnp.int32, (LANES, LANES), 1)
    for row in range(lists):
        mine = jnp.broadcast_to(keys[:, row:row + 1], (LANES, LANES))
        value = jnp.broadcast_to(ranks[:, row:row + 1], (LANES, LANES)) + 1
        for kind in range(len(STAGES) + 1):
            line = jnp.sum(jnp.where(mine == kind * LANES + lane, value, 0), axis=0, keepdims=True)
            if kind == len(STAGES):
                left = jnp.sum(jnp.where(mine >= kind * LANES, 1, 0), axis=0, keepdims=True)
                line = jnp.where(lane[0:1] == LANES - 1, left, line)
            table[kind * 8 + row:kind * 8 + row + 1] = line


def gather_kernel(
    q_hbm, k_ref, v_ref, blocks, counts, win, acc_out, total_out, shift_out, rest_out,
    buf_a, buf_b, buf_c, q_ref, scores, shift, total, acc, pad, flat, table, slots,
    stage, side_sem, out_sem, own_sem, send_sem, recv_sem, sib_send, sib_recv,
):
    g, y, x, core, cross_up, cross_down = position()
    up, down = (g + 1) % GROUPS, (g + GROUPS - 1) % GROUPS
    lists = q_ref.shape[0] // BLOCK
    buffers = (buf_a, buf_b, buf_c)

    def place(px, py):
        return (py * XS + px) * 2 + core

    target = {
        "xp": (g, place((x + XS - 1) % XS, y)),
        "xm": (g, place((x + 1) % XS, y)),
        "y": (g, place(x, 1 - y)),
        "zp": (down, place(x, (y + cross_down) % 2)),
        "zm": (up, place(x, (y + cross_up) % 2)),
    }
    sibling = (g, (y * XS + x) * 2 + 1 - core)

    def spot(piece, side, c):
        order = ORDER.index(piece)
        for (first, end, _), buf in zip(STAGES, buffers):
            if first <= order < end:
                return buf.at[((order - first) * 2 + side) * CH + c]
        return win.at[(order * 2 + side) * CH + c]

    def at(piece, c):
        return spot(piece, core, c)

    def source(piece, c):
        return stage.at[c] if piece == ORDER[0] else at(piece, c)

    def link_copy(link, piece, c, t):
        n = LINKS.index(link)
        return pltpu.make_async_remote_copy(
            src_ref=source(parent(link, piece), c),
            dst_ref=at(piece, c),
            send_sem=send_sem.at[n, t],
            recv_sem=recv_sem.at[n, t],
            device_id=target[link],
            device_id_type=MESH,
        )

    def sib_copy(piece, c, n, t):
        return pltpu.make_async_remote_copy(
            src_ref=source(piece, c),
            dst_ref=at(piece, c),
            send_sem=sib_send.at[n, t],
            recv_sem=sib_recv.at[n, t],
            device_id=sibling,
            device_id_type=MESH,
        )

    def sib_arrival(piece, c, n, t):
        here = spot(piece, 1 - core, c)
        return pltpu.make_async_remote_copy(
            src_ref=here,
            dst_ref=here,
            send_sem=sib_send.at[n, t],
            recv_sem=sib_recv.at[n, t],
            device_id=sibling,
            device_id_type=MESH,
        )

    barrier = pltpu.get_barrier_semaphore()
    for device in (*target.values(), sibling):
        pl.semaphore_signal(barrier, inc=1, device_id=device, device_id_type=MESH)
    q_copy = pltpu.make_async_copy(q_hbm, q_ref, side_sem.at[0])
    q_copy.start()
    fill = []
    for c in range(CH):
        rows = pl.ds(c * BLOCK, BLOCK)
        stage[c, 0] = k_ref[rows]
        stage[c, 1] = v_ref[rows].T
        copy = pltpu.make_async_copy(stage.at[c], at(ORDER[0], c), own_sem.at[c])
        copy.start()
        fill.append(copy)
    pl.semaphore_wait(barrier, len(target) + 1)

    def row(step, c):
        if step < len(STEPS):
            return [(link, STEPS[step][link], c) for link in LINKS]
        return LAST[c]

    def tick(step, c):
        t = step * CH + c
        if isinstance(t, int) and t < CH:
            arrived = ()
        else:
            arrived = row(step - 1, c)
        for link, piece, chunk in arrived:
            link_copy(link, piece, chunk, t - CH).wait_recv()
        for link, piece, chunk in row(step, c) if not (step == len(STEPS) and c >= len(LAST)) else ():
            if not (isinstance(t, int) and t < AHEAD):
                link_copy(link, piece, chunk, t - AHEAD).wait_send()
            link_copy(link, piece, chunk, t).start()
        for link, piece, chunk in arrived:
            sib_copy(piece, chunk, LINKS.index(link), t - CH).start()
        if step == 0:
            sib_copy(ORDER[0], c, len(LINKS), t).start()

    for c in range(CH):
        tick(0, c)

    sort_lists(blocks, counts, lists, pad, flat, table)
    table_copy = pltpu.make_async_copy(table, slots, side_sem.at[1])
    table_copy.start()
    total[...] = jnp.zeros_like(total)
    acc[...] = jnp.zeros_like(acc)
    q_copy.wait()

    def peaks(row, _):
        own = k_ref[pl.ds(pl.multiple_of(row * BLOCK, BLOCK), BLOCK)]
        for t, c in tiles():
            s = nt_dot(own, query_tile(q_ref, row, t))
            shift[row, :, c] = jnp.broadcast_to(jnp.max(s, axis=0, keepdims=True) * SCALE, (8, TILE))
        return 0

    def early(c, _):
        tick(1, c)
        peaks(c, 0)
        return 0

    lax.fori_loop(0, CH, early, 0)
    lax.fori_loop(0, CH, lambda c, _: (tick(2, c), 0)[1], 0)
    table_copy.wait()
    for copy in fill:
        copy.wait()

    def from_sibling(step):
        def one(c, _):
            for link, piece, chunk in row(step, c):
                sib_arrival(piece, chunk, LINKS.index(link), step * CH + c).wait_recv()
            if step == 0:
                sib_arrival(ORDER[0], c, len(LINKS), c).wait_recv()
            return 0

        lax.fori_loop(0, CH, one, 0)

    exports = []

    def export(kind):
        first, end, _ = STAGES[kind]
        blocks_in = 2 * CH * (end - first)
        copy = pltpu.make_async_copy(
            buffers[kind], win.at[pl.ds(2 * CH * first, blocks_in)], out_sem.at[kind]
        )
        copy.start()
        exports.append(copy)

    def take(kind, meanwhile):
        first, _, entries = STAGES[kind]
        buf = buffers[kind]
        subs = entries // STEP

        def codes(row, sub):
            return [slots[kind * 8 + row, sub * STEP + e] for e in range(STEP)]

        def picked(code):
            return [jnp.maximum(n - 1 - 2 * CH * first, 0) for n in code]

        def keys_of(row, sub):
            return jnp.concatenate([buf[n, 0] for n in picked(codes(row, sub))], axis=0)

        ahead(keys_of(0, 0), q_ref, 0, scores)

        def one(row, _):
            meanwhile(row)
            for sub in range(subs):
                code = codes(row, sub)
                v = jnp.concatenate([buf[n, 1] for n in picked(code)], axis=1)
                if sub + 1 < subs:
                    next_row, next_sub = row, sub + 1
                else:
                    next_row, next_sub = jnp.minimum(row + 1, lists - 1), 0
                attend_step(
                    q_ref, scores, shift, total, acc, row, [n > 0 for n in code], v,
                    next_row, keys_of(next_row, next_sub),
                )
            return 0

        lax.fori_loop(0, lists, one, 0)

    from_sibling(0)
    from_sibling(1)
    export(0)
    take(0, lambda c: tick(3, c))
    from_sibling(2)
    export(1)
    for c in range(CH):
        tick(len(STEPS), c)
    take(1, lambda c: None)
    from_sibling(3)
    export(2)
    for c, last in enumerate(LAST):
        t = TICKS - len(LAST) + c
        for link, piece, chunk in last:
            link_copy(link, piece, chunk, t).wait_recv()
            sib_copy(piece, chunk, LINKS.index(link), t).start()
    take(2, lambda c: None)
    results = []
    for n, (src, dst) in enumerate(
        ((acc, acc_out), (total, total_out), (shift, shift_out), (table.at[pl.ds(8 * len(STAGES), 8)], rest_out))
    ):
        copy = pltpu.make_async_copy(src, dst, out_sem.at[len(STAGES) + n])
        copy.start()
        results.append(copy)

    sent = {link: [] for link in LINKS}
    for t in range(TICKS):
        for link, piece, chunk in row(t // CH, t % CH):
            if t >= AHEAD:
                sent[link].remove(t - AHEAD)
            sent[link].append(t)
    for link in LINKS:
        for t in sent[link]:
            link_copy(link, ORDER[1], 0, t).wait_send()

    def drain(c, _):
        for step in range(len(STEPS)):
            for link, piece, chunk in row(step, c):
                sib_copy(piece, chunk, LINKS.index(link), step * CH + c).wait_send()
        sib_copy(ORDER[0], c, len(LINKS), c).wait_send()
        return 0

    lax.fori_loop(0, CH, drain, 0)
    for c, last in enumerate(LAST):
        for link, piece, chunk in last:
            t = TICKS - len(LAST) + c
            sib_copy(piece, chunk, LINKS.index(link), t).wait_send()
            sib_arrival(piece, chunk, LINKS.index(link), t).wait_recv()


    for copy in exports + results:
        copy.wait()


def gather(queries, keys, values, blocks, counts):
    lists = queries.shape[0] // BLOCK
    rows = HEADS * BLOCK
    state = (
        jax.ShapeDtypeStruct((lists, HD, rows), jnp.float32),
        jax.ShapeDtypeStruct((lists, 8, rows), jnp.float32),
        jax.ShapeDtypeStruct((lists, 8, rows), jnp.float32),
    )
    vmem = pl.BlockSpec(memory_space=pltpu.VMEM)
    kinds = len(STAGES)
    return pl.pallas_call(
        gather_kernel,
        out_shape=(
            jax.ShapeDtypeStruct((len(ORDER) * 2 * CH, 2, BLOCK, HD), jnp.bfloat16),
            *state,
            jax.ShapeDtypeStruct((8, LANES), jnp.int32),
        ),
        in_specs=[
            pl.BlockSpec(memory_space=pl.ANY), vmem, vmem, vmem, pl.BlockSpec(memory_space=pltpu.SMEM),
        ],
        out_specs=(pl.BlockSpec(memory_space=pl.ANY),) * 5,
        scratch_shapes=[
            *(pltpu.VMEM((2 * CH * (end - first), 2, BLOCK, HD), jnp.bfloat16) for first, end, _ in STAGES),
            pltpu.VMEM(queries.shape, queries.dtype),
            pltpu.VMEM((STEP * BLOCK, rows), jnp.float32),
            pltpu.VMEM((lists, 8, rows), jnp.float32),
            pltpu.VMEM((lists, 8, rows), jnp.float32),
            pltpu.VMEM((lists, HD, rows), jnp.float32),
            pltpu.VMEM((8, LANES), jnp.int32),
            pltpu.VMEM((LANES, LANES), jnp.int32),
            pltpu.VMEM((8 * (kinds + 1), LANES), jnp.int32),
            pltpu.SMEM((8 * (kinds + 1), LANES), jnp.int32),
            pltpu.VMEM((CH, 2, BLOCK, HD), jnp.bfloat16),
            pltpu.SemaphoreType.DMA((2,)),
            pltpu.SemaphoreType.DMA((kinds + 4,)),
            pltpu.SemaphoreType.DMA((CH,)),
            pltpu.SemaphoreType.DMA((len(LINKS), TICKS)),
            pltpu.SemaphoreType.DMA((len(LINKS), TICKS)),
            pltpu.SemaphoreType.DMA((len(LINKS) + 1, TICKS)),
            pltpu.SemaphoreType.DMA((len(LINKS) + 1, TICKS)),
        ],
        compiler_params=pltpu.CompilerParams(
            collective_id=0, has_side_effects=True, vmem_limit_bytes=VMEM_LIMIT
        ),
    )(queries, keys, values, blocks, counts)


def rest_kernel(
    rest, blocks, counts, q_hbm, win, acc_hbm, total_hbm, shift_hbm, o_hbm,
    kv, q_ref, scores, shift, total, total_in, acc, acc_in, out, places, rows_of, sem, side_sem, out_sem,
):
    g, y, x, _, cross_up, cross_down = position()
    lists = q_ref.shape[0] // BLOCK
    q_copy = pltpu.make_async_copy(q_hbm, q_ref, side_sem.at[0])
    shift_copy = pltpu.make_async_copy(shift_hbm, shift, side_sem.at[1])
    total_copy = pltpu.make_async_copy(total_hbm, total_in, side_sem.at[2])
    acc_copy = pltpu.make_async_copy(acc_hbm, acc_in, side_sem.at[3])

    def fetch(n, e, source):
        return pltpu.make_async_copy(win.at[source], kv.at[n, e], sem.at[n, e])

    def plan(row, n):
        def one(s, n):
            rows_of[n, STEP] = row
            for e in range(STEP):
                code = rest[row, s * STEP + e]
                rows_of[n, e] = code
                fetch(n, e, jnp.maximum(code - 1, 0)).start()
            return n + 1

        return lax.fori_loop(0, (rest[row, LANES - 1] + STEP - 1) // STEP, one, n)

    q_copy.start()
    steps = lax.fori_loop(0, lists, plan, 0)
    for copy in (shift_copy, total_copy, acc_copy):
        copy.start()
    total[...] = jnp.zeros_like(total)
    acc[...] = jnp.zeros_like(acc)

    def wait(n):
        for e in range(STEP):
            fetch(n, e, 0).wait()

    def keys_of(n):
        return jnp.concatenate([kv[n, e, 0] for e in range(STEP)], axis=0)

    q_copy.wait()

    @pl.when(steps > 0)
    def _():
        wait(0)
        ahead(keys_of(0), q_ref, rows_of[0, STEP], scores)

    shift_copy.wait()

    def step(n, _):
        following = jnp.minimum(n + 1, steps - 1)

        @pl.when(n + 1 < steps)
        def _():
            wait(n + 1)

        v = jnp.concatenate([kv[n, e, 1] for e in range(STEP)], axis=1)
        attend_step(
            q_ref, scores, shift, total, acc, rows_of[n, STEP], [rows_of[n, e] > 0 for e in range(STEP)], v,
            rows_of[following, STEP], keys_of(following),
        )
        return 0

    lax.fori_loop(0, steps, step, 0)
    total_copy.wait()
    acc_copy.wait()

    def rank(block):
        group = (block // GROUP_BLOCKS - g + 1 + GROUPS) % GROUPS
        device = block % GROUP_BLOCKS // CH
        turn = jnp.where(group == 2, cross_up, jnp.where(group == 0, cross_down, 0))
        dx = (device // 2 % XS - x + XS) % XS
        dy = (device // (2 * XS) + y + turn) % 2
        return (places[group * 2 * XS + dy * XS + dx] * 2 + device % 2) * CH + block % CH

    def finish(row, _):
        acc[row] += acc_in[row]
        total[row] += total_in[row]
        safe = jnp.max(jnp.sum(total[row], axis=0, keepdims=True)) < LIMIT

        @pl.when(jnp.logical_not(safe))
        def _():
            for i, (dx, dy, dz) in enumerate(ORDER):
                places[(dz + 1) * 2 * XS + dy * XS + dx] = i
            for t, c in tiles():
                q = query_tile(q_ref, row, t)

                def one(e, state, q=q):
                    peak, tot, mixed = state
                    copy = fetch(0, 0, rank(blocks[row, e]))
                    copy.start()
                    copy.wait()
                    s = nt_dot(kv[0, 0, 0], q) * SCALE
                    new = jnp.maximum(peak, jnp.max(s, axis=0, keepdims=True))
                    weights = jnp.exp2(s - new)
                    keep = jnp.exp2(peak - new)
                    tot = tot * keep + jnp.sum(weights, axis=0, keepdims=True)
                    mixed = mixed * keep + jnp.dot(
                        kv[0, 0, 1], weights.astype(jnp.bfloat16), preferred_element_type=jnp.float32
                    )
                    return new, tot, mixed

                start = (
                    jnp.full((1, TILE), -DEAD, jnp.float32),
                    jnp.zeros((1, TILE), jnp.float32),
                    jnp.zeros((HD, TILE), jnp.float32),
                )
                _, tot, mixed = lax.fori_loop(0, counts[row], one, start)
                total[row, :, c] = jnp.concatenate([tot, jnp.zeros((7, TILE), jnp.float32)], axis=0)
                acc[row, :, c] = mixed

        scale = 1.0 / jnp.sum(total[row], axis=0, keepdims=True)
        rows = pl.ds(pl.multiple_of(row * BLOCK, BLOCK), BLOCK)
        for h in range(HEADS):
            c = slice(h * HD, (h + 1) * HD)
            out[rows, c] = (acc[row, :, c] * scale[:, c]).astype(jnp.bfloat16).T
        pltpu.make_async_copy(out.at[rows], o_hbm.at[rows], out_sem.at[row]).start()
        return 0

    lax.fori_loop(0, lists, finish, 0)

    def sent(row, _):
        rows = pl.ds(pl.multiple_of(row * BLOCK, BLOCK), BLOCK)
        pltpu.make_async_copy(out.at[rows], o_hbm.at[rows], out_sem.at[row]).wait()
        return 0

    lax.fori_loop(0, lists, sent, 0)


def attend_rest(rest, blocks, counts, queries, window, acc, total, shift):
    lists = queries.shape[0] // BLOCK
    steps = lists * (MAXB // STEP)
    rows = HEADS * BLOCK
    hbm = pl.BlockSpec(memory_space=pl.ANY)
    return pl.pallas_call(
        rest_kernel,
        in_specs=[pl.BlockSpec(memory_space=pltpu.SMEM)] * 3 + [hbm] * 5,
        out_specs=hbm,
        scratch_shapes=[
            pltpu.VMEM((steps, STEP, 2, BLOCK, HD), jnp.bfloat16),
            pltpu.VMEM(queries.shape, queries.dtype),
            pltpu.VMEM((STEP * BLOCK, rows), jnp.float32),
            *[pltpu.VMEM((lists, 8, rows), jnp.float32)] * 3,
            *[pltpu.VMEM((lists, HD, rows), jnp.float32)] * 2,
            pltpu.VMEM(queries.shape, queries.dtype),
            pltpu.SMEM((len(ORDER),), jnp.int32),
            pltpu.SMEM((steps, STEP + 1), jnp.int32),
            pltpu.SemaphoreType.DMA((steps, STEP)),
            pltpu.SemaphoreType.DMA((4,)),
            pltpu.SemaphoreType.DMA((lists,)),
        ],
        out_shape=jax.ShapeDtypeStruct(queries.shape, jnp.bfloat16),
        compiler_params=pltpu.CompilerParams(vmem_limit_bytes=VMEM_LIMIT),
    )(rest, blocks, counts, queries, window, acc, total, shift)


def body(queries, keys, values, key_blocks, key_counts):
    window, acc, total, shift, rest = gather(queries, keys, values, key_blocks, key_counts)
    return attend_rest(rest, key_blocks, key_counts, queries, window, acc, total, shift)


def solution(mesh):
    placed = (
        P(("outer", "inner"), None),
        P(("outer", "inner"), None),
        P(("outer", "inner"), None),
        P(("outer", "inner"), None),
        P(("outer", "inner")),
    )
    return jax.shard_map(
        body, mesh=mesh, in_specs=placed, out_specs=P(("outer", "inner"), None), check_vma=False
    )
```

```python
import functools

import jax
import jax.numpy as jnp
from jax import lax
from jax.experimental import pallas as pl
from jax.experimental.pallas import tpu as pltpu
from jax.sharding import PartitionSpec as P

HD = 128
HEADS = 8
BLOCK = 128
MAXB = 44
XS = 4
ZS = 8
CH = 4
GROUP_BLOCKS = 64
STEP = 4
TILE = 2 * HD
GROUPS = 16
SCALE = HD ** -0.5 * 1.4426950408889634
LIMIT = 2.0 ** 100
DEAD = 1e30
LANES = 128
VMEM_LIMIT = 60 * 2 ** 20
MESH = pl.DeviceIdType.MESH

LINKS = ("xp", "xm", "y", "zp", "zm")
STEPS = (
    {"xp": (1, 0, 0), "xm": (3, 0, 0), "y": (0, 1, 0), "zp": (0, 0, 1), "zm": (0, 0, -1)},
    {"xp": (2, 0, 0), "xm": (3, 0, 1), "y": (1, 1, 0), "zp": (1, 0, 1), "zm": (3, 0, -1)},
    {"xp": (1, 0, -1), "xm": (3, 1, 0), "y": (2, 1, 0), "zp": (0, 1, 1), "zm": (0, 1, -1)},
    {"xp": (2, 0, 1), "xm": (2, 0, -1), "y": (3, 1, 1), "zp": (1, 1, 1), "zm": (1, 1, -1)},
)
LAST = (
    (("xm", (3, 1, -1), 0), ("y", (3, 1, -1), 2), ("zp", (2, 1, 1), 1), ("zm", (2, 1, -1), 1)),
    (("xp", (2, 1, 1), 0), ("xm", (3, 1, -1), 1), ("y", (3, 1, -1), 3), ("zp", (2, 1, 1), 2), ("zm", (2, 1, -1), 2)),
    (("y", (2, 1, -1), 0), ("zp", (2, 1, 1), 3), ("zm", (2, 1, -1), 3)),
)
ORDER = ((0, 0, 0),) + tuple(row[link] for row in STEPS for link in LINKS) + ((3, 1, -1), (2, 1, 1), (2, 1, -1))
STAGES = ((0, 6, 8), (6, 11, 8), (11, 16, 8), (16, 21, 4))
TICKS = CH * len(STEPS) + len(LAST)
AHEAD = 4


def parent(link, piece):
    dx, dy, dz = piece
    return {
        "xp": ((dx + XS - 1) % XS, dy, dz),
        "xm": ((dx + 1) % XS, dy, dz),
        "y": (dx, 1 - dy, dz),
        "zp": (dx, dy, dz - 1),
        "zm": (dx, dy, dz + 1),
    }[link]


def position():
    g = lax.axis_index("outer")
    inner = lax.axis_index("inner")
    cross_up = jnp.where(g % ZS == ZS - 1, 1, 0)
    cross_down = jnp.where(g % ZS == 0, 1, 0)
    return g, inner // (2 * XS), inner // 2 % XS, inner % 2, cross_up, cross_down


def nt_dot(a, b):
    return lax.dot_general(a, b, (((1,), (1,)), ((), ())), preferred_element_type=jnp.float32)


def query_tile(q_ref, row, t):
    rows = pl.ds(pl.multiple_of(row * BLOCK, BLOCK), BLOCK)
    return jnp.concatenate([q_ref[rows, h * HD:(h + 1) * HD] for h in (2 * t, 2 * t + 1)], axis=0)


def tiles():
    return [(t, pl.ds(t * TILE, TILE)) for t in range(HEADS * HD // TILE)]


def ahead(k_ref, q_ref, row, scores):
    for t, c in tiles():
        scores[:, c] = nt_dot(k_ref, query_tile(q_ref, row, t))


def attend_step(q_ref, scores, shift, total, acc, row, live, v, next_row, next_k):
    for t, c in tiles():
        base = shift[row, 0:1, c]
        parts = []
        for e in range(STEP):
            m = jnp.where(live[e], base, DEAD)
            parts.append(jnp.exp2(scores[pl.ds(e * BLOCK, BLOCK), c] * SCALE - m))
        scores[:, c] = nt_dot(next_k, query_tile(q_ref, next_row, t))
        weights = jnp.concatenate(parts, axis=0)
        total[row, :, c] += jnp.sum(weights.reshape(STEP * BLOCK // 8, 8, TILE), axis=0)
        acc[row, :, c] += jnp.dot(v, weights.astype(jnp.bfloat16), preferred_element_type=jnp.float32)


def sort_lists(blocks, counts, lists, pad, flat, table):
    g, y, x, _, cross_up, cross_down = position()
    pad[...] = jnp.zeros_like(pad)
    pad[0:lists, 0:MAXB] = blocks[...]
    block = pad[...]
    lane = lax.broadcasted_iota(jnp.int32, (8, LANES), 1)
    line = lax.broadcasted_iota(jnp.int32, (8, LANES), 0)
    length = jnp.zeros((8, LANES), jnp.int32)
    for row in range(lists):
        length = jnp.where(line == row, counts[row], length)
    group = (block // GROUP_BLOCKS - g + 1 + GROUPS) % GROUPS
    device = block % GROUP_BLOCKS // CH
    turn = jnp.where(group == 2, cross_up, jnp.where(group == 0, cross_down, 0))
    dx = (device // 2 % XS - x + XS) % XS
    dy = (device // (2 * XS) + y + turn) % 2
    code = group * 2 * XS + dy * XS + dx
    order = jnp.zeros_like(code)
    for i, (px, py, pz) in enumerate(ORDER):
        order = jnp.where(code == (pz + 1) * 2 * XS + py * XS + px, i, order)
    rank = (order * 2 + device % 2) * CH + block % CH

    def before(mask):
        ones = jnp.where(mask, 1, 0)
        count = ones
        for k in (1, 2, 4, 8, 16, 32):
            count = count + jnp.where(lane >= k, pltpu.roll(count, k, 1), 0)
        return count - ones

    rest = lane < length
    key = jnp.full((8, LANES), -1, jnp.int32)
    for kind, (first, end, slots) in enumerate(STAGES):
        mask = (lane < length) & (order >= first) & (order < end)
        place = before(mask)
        mask = mask & (place < slots)
        key = jnp.where(mask, kind * LANES + place, key)
        rest = rest & jnp.logical_not(mask)
    key = jnp.where(rest, len(STAGES) * LANES + before(rest), key)
    flat[...] = jnp.full((LANES, LANES), -1, jnp.int32)
    flat[0:8] = key
    keys = flat[...].T
    flat[0:8] = rank
    ranks = flat[...].T
    lane = lax.broadcasted_iota(jnp.int32, (LANES, LANES), 1)
    for row in range(lists):
        mine = jnp.broadcast_to(keys[:, row:row + 1], (LANES, LANES))
        value = jnp.broadcast_to(ranks[:, row:row + 1], (LANES, LANES)) + 1
        for kind in range(len(STAGES) + 1):
            line = jnp.sum(jnp.where(mine == kind * LANES + lane, value, 0), axis=0, keepdims=True)
            if kind == len(STAGES):
                left = jnp.sum(jnp.where(mine >= kind * LANES, 1, 0), axis=0, keepdims=True)
                line = jnp.where(lane[0:1] == LANES - 1, left, line)
            table[kind * 8 + row:kind * 8 + row + 1] = line


def gather_kernel(
    q_hbm, k_hbm, v_hbm, blocks, counts, win, acc_out, total_out, shift_out, rest_out,
    buf_a, buf_b, buf_c, buf_d, q_ref, v_ref, scores, shift, total, acc, pad, flat, table, slots,
    stage, in_sem, side_sem, out_sem, own_sem, send_sem, recv_sem, sib_send, sib_recv,
):
    g, y, x, core, cross_up, cross_down = position()
    up, down = (g + 1) % GROUPS, (g + GROUPS - 1) % GROUPS
    lists = q_ref.shape[0] // BLOCK
    buffers = (buf_a, buf_b, buf_c, buf_d)

    def place(px, py):
        return (py * XS + px) * 2 + core

    target = {
        "xp": (g, place((x + XS - 1) % XS, y)),
        "xm": (g, place((x + 1) % XS, y)),
        "y": (g, place(x, 1 - y)),
        "zp": (down, place(x, (y + cross_down) % 2)),
        "zm": (up, place(x, (y + cross_up) % 2)),
    }
    sibling = (g, (y * XS + x) * 2 + 1 - core)

    def part(order, side, c, blocks):
        for (first, end, _), buf in zip(STAGES, buffers):
            if first <= order < end:
                return buf.at[pl.ds(((order - first) * 2 + side) * CH + c, blocks)]
        return win.at[pl.ds((order * 2 + side) * CH + c, blocks)]

    def at(piece, c):
        return part(ORDER.index(piece), core, c, 1)

    def source(piece, c):
        return stage.at[pl.ds(c, 1)] if piece == ORDER[0] else at(piece, c)

    def remote(src, dst, send, recv, device):
        return pltpu.make_async_remote_copy(
            src_ref=src, dst_ref=dst, send_sem=send, recv_sem=recv, device_id=device, device_id_type=MESH
        )

    def link_copy(link, piece, c, t):
        return remote(
            source(parent(link, piece), c), at(piece, c), send_sem.at[t], recv_sem.at[t], target[link]
        )

    def sib_copy(piece, c, n, blocks):
        side = core
        order = ORDER.index(piece)
        if piece == ORDER[0]:
            src = stage.at[pl.ds(c, blocks)]
        else:
            src = part(order, side, c, blocks)
        return remote(src, part(order, side, c, blocks), sib_send.at[n], sib_recv.at[n], sibling)

    def many(blocks, sems, n):
        some = buf_a.at[pl.ds(0, blocks)]
        return remote(some, some, sems[0].at[n], sems[1].at[n], sibling)

    links, sibs = (send_sem, recv_sem), (sib_send, sib_recv)
    last_sib = 1 + 2 * len(STEPS)

    barrier = pltpu.get_barrier_semaphore()
    for device in (*target.values(), sibling):
        pl.semaphore_signal(barrier, inc=1, device_id=device, device_id_type=MESH)
    k_copies, v_copies, fill = [], [], []
    for c in range(CH):
        rows = pl.ds(c * BLOCK, BLOCK)
        k_copies.append(pltpu.make_async_copy(k_hbm.at[rows], stage.at[c, 0], in_sem.at[0, c]))
        v_copies.append(pltpu.make_async_copy(v_hbm.at[rows], v_ref.at[c], in_sem.at[1, c]))
        k_copies[c].start()
        v_copies[c].start()
    q_copy = pltpu.make_async_copy(q_hbm, q_ref, side_sem.at[0])
    q_copy.start()
    for c in range(CH):
        v_copies[c].wait()
        stage[c, 1] = v_ref[c].T
        k_copies[c].wait()
        copy = pltpu.make_async_copy(stage.at[pl.ds(c, 1)], at(ORDER[0], c), own_sem.at[c])
        copy.start()
        fill.append(copy)
    pl.semaphore_wait(barrier, len(target) + 1)

    def row(step, c):
        if step < len(STEPS):
            return [(link, STEPS[step][link], c) for link in LINKS]
        return LAST[c]

    def when(condition, run):
        if isinstance(condition, bool):
            if condition:
                run()
        else:
            pl.when(condition)(run)

    def tick(step, c):
        t = step * CH + c
        now = row(step, c) if step < len(STEPS) or c < len(LAST) else ()
        late = [step == 1 or (link == "y" and step == 2) for link, _, _ in now]
        if now and step * CH >= AHEAD:
            if step < len(STEPS) or not isinstance(t, int):
                many(len(LINKS), links, t - AHEAD).wait_send()
            else:
                many(len(row((t - AHEAD) // CH, (t - AHEAD) % CH)), links, t - AHEAD).wait_send()
        for after in (False, True):
            if after and step > 0:
                many(len(LINKS), links, t - CH).wait_recv()
            for (link, piece, chunk), tardy in zip(now, late):
                if tardy == after:
                    link_copy(link, piece, chunk, t).start()
        if step > 0:
            def forward():
                for link, piece, _ in row(step - 1, c):
                    sib_copy(piece, c - 1, 1 + 2 * (step - 1) + c // 2, 2).start()

            when(c % 2 == 1, forward)

    for c in range(CH):
        tick(0, c)
    sib_copy(ORDER[0], 0, 0, CH).start()

    sort_lists(blocks, counts, lists, pad, flat, table)
    table_copy = pltpu.make_async_copy(table, slots, side_sem.at[1])
    table_copy.start()
    total[...] = jnp.zeros_like(total)
    acc[...] = jnp.zeros_like(acc)
    q_copy.wait()

    def peaks(row, _):
        own = stage[row, 0]
        for t, c in tiles():
            s = nt_dot(own, query_tile(q_ref, row, t))
            shift[row, :, c] = jnp.broadcast_to(jnp.max(s, axis=0, keepdims=True) * SCALE, (8, TILE))
        return 0

    def early(c, _):
        tick(1, c)
        peaks(c, 0)
        return 0

    lax.fori_loop(0, CH, early, 0)
    table_copy.wait()
    for copy in fill:
        copy.wait()

    def from_sibling(step):
        if step == 0:
            many(CH, sibs, 0).wait_recv()
        for half in range(2):
            many(2 * len(LINKS), sibs, 1 + 2 * step + half).wait_recv()

    exports = []

    def export(kind):
        first, end, _ = STAGES[kind]
        blocks_in = 2 * CH * (end - first)
        copy = pltpu.make_async_copy(
            buffers[kind], win.at[pl.ds(2 * CH * first, blocks_in)], out_sem.at[kind]
        )
        copy.start()
        exports.append(copy)

    def take(kind, meanwhile):
        first, _, entries = STAGES[kind]
        buf = buffers[kind]
        subs = entries // STEP

        def codes(row, sub):
            return [slots[kind * 8 + row, sub * STEP + e] for e in range(STEP)]

        def picked(code):
            return [jnp.maximum(n - 1 - 2 * CH * first, 0) for n in code]

        def keys_of(row, sub):
            return jnp.concatenate([buf[n, 0] for n in picked(codes(row, sub))], axis=0)

        ahead(keys_of(0, 0), q_ref, 0, scores)

        def one(row, _):
            meanwhile(row)
            for sub in range(subs):
                code = codes(row, sub)
                v = jnp.concatenate([buf[n, 1] for n in picked(code)], axis=1)
                if sub + 1 < subs:
                    next_row, next_sub = row, sub + 1
                else:
                    next_row, next_sub = jnp.minimum(row + 1, lists - 1), 0
                attend_step(
                    q_ref, scores, shift, total, acc, row, [n > 0 for n in code], v,
                    next_row, keys_of(next_row, next_sub),
                )
            return 0

        lax.fori_loop(0, lists, one, 0)

    for kind in range(len(STAGES)):
        from_sibling(kind)
        export(kind)
        if kind + 2 < len(STAGES):
            take(kind, lambda c, kind=kind: tick(kind + 2, c))
        elif kind + 2 == len(STAGES):
            for c in range(CH):
                tick(len(STEPS), c)
            take(kind, lambda c: None)
        else:
            take(kind, lambda c: None)
    results = []
    for n, (src, dst) in enumerate(
        ((acc, acc_out), (total, total_out), (shift, shift_out), (table.at[pl.ds(8 * len(STAGES), 8)], rest_out))
    ):
        copy = pltpu.make_async_copy(src, dst, out_sem.at[len(STAGES) + n])
        copy.start()
        results.append(copy)

    for c, last in enumerate(LAST):
        many(len(last), links, len(STEPS) * CH + c).wait_recv()
        for link, piece, chunk in last:
            sib_copy(piece, chunk, last_sib + c, 1).start()
    for t in range(TICKS - AHEAD, TICKS):
        many(len(row(t // CH, t % CH)), links, t).wait_send()
    many(CH, sibs, 0).wait_send()
    for n in range(1, last_sib):
        many(2 * len(LINKS), sibs, n).wait_send()
    for c, last in enumerate(LAST):
        many(len(last), sibs, last_sib + c).wait_send()
        many(len(last), sibs, last_sib + c).wait_recv()
    for copy in exports + results:
        copy.wait()


def gather(queries, keys, values, blocks, counts):
    lists = queries.shape[0] // BLOCK
    rows = HEADS * BLOCK
    state = (
        jax.ShapeDtypeStruct((lists, HD, rows), jnp.float32),
        jax.ShapeDtypeStruct((lists, 8, rows), jnp.float32),
        jax.ShapeDtypeStruct((lists, 8, rows), jnp.float32),
    )
    vmem = pl.BlockSpec(memory_space=pltpu.VMEM)
    kinds = len(STAGES)
    return pl.pallas_call(
        gather_kernel,
        out_shape=(
            jax.ShapeDtypeStruct((len(ORDER) * 2 * CH, 2, BLOCK, HD), jnp.bfloat16),
            *state,
            jax.ShapeDtypeStruct((8, LANES), jnp.int32),
        ),
        in_specs=[
            *[pl.BlockSpec(memory_space=pl.ANY)] * 3, vmem, pl.BlockSpec(memory_space=pltpu.SMEM),
        ],
        out_specs=(pl.BlockSpec(memory_space=pl.ANY),) * 5,
        scratch_shapes=[
            *(pltpu.VMEM((2 * CH * (end - first), 2, BLOCK, HD), jnp.bfloat16) for first, end, _ in STAGES),
            pltpu.VMEM(queries.shape, queries.dtype),
            pltpu.VMEM((CH, BLOCK, HD), jnp.bfloat16),
            pltpu.VMEM((STEP * BLOCK, rows), jnp.float32),
            pltpu.VMEM((lists, 8, rows), jnp.float32),
            pltpu.VMEM((lists, 8, rows), jnp.float32),
            pltpu.VMEM((lists, HD, rows), jnp.float32),
            pltpu.VMEM((8, LANES), jnp.int32),
            pltpu.VMEM((LANES, LANES), jnp.int32),
            pltpu.VMEM((8 * (kinds + 1), LANES), jnp.int32),
            pltpu.SMEM((8 * (kinds + 1), LANES), jnp.int32),
            pltpu.VMEM((CH, 2, BLOCK, HD), jnp.bfloat16),
            pltpu.SemaphoreType.DMA((2, CH)),
            pltpu.SemaphoreType.DMA((2,)),
            pltpu.SemaphoreType.DMA((kinds + 4,)),
            pltpu.SemaphoreType.DMA((CH,)),
            pltpu.SemaphoreType.DMA((TICKS,)),
            pltpu.SemaphoreType.DMA((TICKS,)),
            pltpu.SemaphoreType.DMA((1 + 2 * len(STEPS) + len(LAST),)),
            pltpu.SemaphoreType.DMA((1 + 2 * len(STEPS) + len(LAST),)),
        ],
        compiler_params=pltpu.CompilerParams(
            collective_id=0, has_side_effects=True, vmem_limit_bytes=VMEM_LIMIT
        ),
    )(queries, keys, values, blocks, counts)


def rest_kernel(
    rest, blocks_hbm, counts_hbm, q_hbm, win, acc_hbm, total_hbm, shift_hbm, o_hbm,
    kv, q_ref, scores, shift, total, acc, out, blocks, counts, places, plan, sem, side_sem, out_sem,
):
    g, y, x, _, cross_up, cross_down = position()
    lists = q_ref.shape[0] // BLOCK
    q_copy = pltpu.make_async_copy(q_hbm, q_ref, side_sem.at[0])
    shift_copy = pltpu.make_async_copy(shift_hbm, shift, side_sem.at[1])
    total_copy = pltpu.make_async_copy(total_hbm, total, side_sem.at[2])
    acc_copy = pltpu.make_async_copy(acc_hbm, acc, side_sem.at[3])

    def fetch(n, e, source):
        return pltpu.make_async_copy(win.at[source], kv.at[n, e], sem.at[n, e])

    def plan_list(row, n):
        def one(s, n):
            plan[n, STEP] = row
            for e in range(STEP):
                code = rest[row, s * STEP + e]
                plan[n, e] = code
                fetch(n, e, jnp.maximum(code - 1, 0)).start()
            return n + 1

        return lax.fori_loop(0, (rest[row, LANES - 1] + STEP - 1) // STEP, one, n)

    q_copy.start()
    steps = lax.fori_loop(0, lists, plan_list, 0)
    for copy in (shift_copy, total_copy, acc_copy):
        copy.start()

    def wait(n):
        for e in range(STEP):
            fetch(n, e, 0).wait()

    def keys_of(n):
        return jnp.concatenate([kv[n, e, 0] for e in range(STEP)], axis=0)

    q_copy.wait()

    @pl.when(steps > 0)
    def _():
        wait(0)
        ahead(keys_of(0), q_ref, plan[0, STEP], scores)

    for copy in (shift_copy, total_copy, acc_copy):
        copy.wait()

    def step(n, _):
        following = jnp.minimum(n + 1, steps - 1)

        @pl.when(n + 1 < steps)
        def _():
            wait(n + 1)

        v = jnp.concatenate([kv[n, e, 1] for e in range(STEP)], axis=1)
        attend_step(
            q_ref, scores, shift, total, acc, plan[n, STEP], [plan[n, e] > 0 for e in range(STEP)], v,
            plan[following, STEP], keys_of(following),
        )
        return 0

    lax.fori_loop(0, steps, step, 0)

    def rank(block):
        group = (block // GROUP_BLOCKS - g + 1 + GROUPS) % GROUPS
        device = block % GROUP_BLOCKS // CH
        turn = jnp.where(group == 2, cross_up, jnp.where(group == 0, cross_down, 0))
        dx = (device // 2 % XS - x + XS) % XS
        dy = (device // (2 * XS) + y + turn) % 2
        return (places[group * 2 * XS + dy * XS + dx] * 2 + device % 2) * CH + block % CH

    def again(row, _):
        for t, c in tiles():
            q = query_tile(q_ref, row, t)

            def one(e, state, q=q):
                peak, tot, mixed = state
                copy = fetch(0, 0, rank(blocks[row, e]))
                copy.start()
                copy.wait()
                s = nt_dot(kv[0, 0, 0], q) * SCALE
                new = jnp.maximum(peak, jnp.max(s, axis=0, keepdims=True))
                weights = jnp.exp2(s - new)
                keep = jnp.exp2(peak - new)
                tot = tot * keep + jnp.sum(weights, axis=0, keepdims=True)
                mixed = mixed * keep + jnp.dot(
                    kv[0, 0, 1], weights.astype(jnp.bfloat16), preferred_element_type=jnp.float32
                )
                return new, tot, mixed

            start = (
                jnp.full((1, TILE), -DEAD, jnp.float32),
                jnp.zeros((1, TILE), jnp.float32),
                jnp.zeros((HD, TILE), jnp.float32),
            )
            _, tot, mixed = lax.fori_loop(0, counts[row], one, start)
            total[row, :, c] = jnp.concatenate([tot, jnp.zeros((7, TILE), jnp.float32)], axis=0)
            acc[row, :, c] = mixed
        return 0

    safe = jnp.max(jnp.sum(total[...], axis=1)) < LIMIT

    @pl.when(jnp.logical_not(safe))
    def _():
        for n, (src, dst) in enumerate(((blocks_hbm, blocks), (counts_hbm, counts))):
            copy = pltpu.make_async_copy(src, dst, side_sem.at[n])
            copy.start()
            copy.wait()
        for i, (dx, dy, dz) in enumerate(ORDER):
            places[(dz + 1) * 2 * XS + dy * XS + dx] = i
        lax.fori_loop(0, lists, again, 0)

    def finish(row, _):
        scale = 1.0 / jnp.sum(total[row], axis=0, keepdims=True)
        rows = pl.ds(pl.multiple_of(row * BLOCK, BLOCK), BLOCK)
        for h in range(HEADS):
            c = slice(h * HD, (h + 1) * HD)
            out[rows, c] = (acc[row, :, c] * scale[:, c]).astype(jnp.bfloat16).T
        pltpu.make_async_copy(out.at[rows], o_hbm.at[rows], out_sem.at[row]).start()
        return 0

    lax.fori_loop(0, lists, finish, 0)

    def sent(row, _):
        rows = pl.ds(pl.multiple_of(row * BLOCK, BLOCK), BLOCK)
        pltpu.make_async_copy(out.at[rows], o_hbm.at[rows], out_sem.at[row]).wait()
        return 0

    lax.fori_loop(0, lists, sent, 0)


def attend_rest(rest, blocks, counts, queries, window, acc, total, shift):
    lists = queries.shape[0] // BLOCK
    steps = lists * (MAXB // STEP)
    rows = HEADS * BLOCK
    hbm = pl.BlockSpec(memory_space=pl.ANY)
    return pl.pallas_call(
        rest_kernel,
        in_specs=[pl.BlockSpec(memory_space=pltpu.SMEM)] + [hbm] * 7,
        out_specs=hbm,
        scratch_shapes=[
            pltpu.VMEM((steps, STEP, 2, BLOCK, HD), jnp.bfloat16),
            pltpu.VMEM(queries.shape, queries.dtype),
            pltpu.VMEM((STEP * BLOCK, rows), jnp.float32),
            *[pltpu.VMEM((lists, 8, rows), jnp.float32)] * 2,
            pltpu.VMEM((lists, HD, rows), jnp.float32),
            pltpu.VMEM(queries.shape, queries.dtype),
            pltpu.SMEM(blocks.shape, jnp.int32),
            pltpu.SMEM(counts.shape, jnp.int32),
            pltpu.SMEM((len(ORDER),), jnp.int32),
            pltpu.SMEM((steps, STEP + 1), jnp.int32),
            pltpu.SemaphoreType.DMA((steps, STEP)),
            pltpu.SemaphoreType.DMA((4,)),
            pltpu.SemaphoreType.DMA((lists,)),
        ],
        out_shape=jax.ShapeDtypeStruct(queries.shape, jnp.bfloat16),
        compiler_params=pltpu.CompilerParams(vmem_limit_bytes=VMEM_LIMIT),
    )(rest, blocks, counts, queries, window, acc, total, shift)


def body(queries, keys, values, key_blocks, key_counts):
    window, acc, total, shift, rest = gather(queries, keys, values, key_blocks, key_counts)
    return attend_rest(rest, key_blocks, key_counts, queries, window, acc, total, shift)


def solution(mesh):
    placed = (
        P(("outer", "inner"), None),
        P(("outer", "inner"), None),
        P(("outer", "inner"), None),
        P(("outer", "inner"), None),
        P(("outer", "inner")),
    )
    return jax.shard_map(
        body, mesh=mesh, in_specs=placed, out_specs=P(("outer", "inner"), None), check_vma=False
    )
```

```python
import functools

import jax
import jax.numpy as jnp
from jax import lax
from jax.experimental import pallas as pl
from jax.experimental.pallas import tpu as pltpu
from jax.sharding import PartitionSpec as P

HD = 128
HEADS = 8
BLOCK = 128
MAXB = 44
XS = 4
ZS = 8
CH = 4
GROUP_BLOCKS = 64
STEP = 4
PART = 2
TILE = 2 * HD
GROUPS = 16
SCALE = HD ** -0.5 * 1.4426950408889634
LIMIT = 2.0 ** 100
DEAD = 1e30
LANES = 128
VMEM_LIMIT = 60 * 2 ** 20
MESH = pl.DeviceIdType.MESH

LINKS = ("xp", "xm", "y", "zp", "zm")
STEPS = (
    {"xp": (1, 0, 0), "xm": (3, 0, 0), "y": (0, 1, 0), "zp": (0, 0, 1), "zm": (0, 0, -1)},
    {"xp": (2, 0, 0), "xm": (3, 0, 1), "y": (1, 1, 0), "zp": (1, 0, 1), "zm": (3, 0, -1)},
    {"xp": (1, 0, -1), "xm": (3, 1, 0), "y": (2, 1, 0), "zp": (0, 1, 1), "zm": (0, 1, -1)},
    {"xp": (2, 0, 1), "xm": (2, 0, -1), "y": (3, 1, 1), "zp": (1, 1, 1), "zm": (1, 1, -1)},
)
LAST = (
    (("xm", (3, 1, -1), 0), ("y", (3, 1, -1), 2), ("zp", (2, 1, 1), 1), ("zm", (2, 1, -1), 1)),
    (("xp", (2, 1, 1), 0), ("xm", (3, 1, -1), 1), ("y", (3, 1, -1), 3), ("zp", (2, 1, 1), 2), ("zm", (2, 1, -1), 2)),
    (("y", (2, 1, -1), 0), ("zp", (2, 1, 1), 3), ("zm", (2, 1, -1), 3)),
)
ORDER = ((0, 0, 0),) + tuple(row[link] for row in STEPS for link in LINKS) + ((3, 1, -1), (2, 1, 1), (2, 1, -1))
STAGES = ((0, 6, 8), (6, 11, 8), (11, 16, 8), (16, 21, 4))
TICKS = CH * len(STEPS) + len(LAST)
AHEAD = 4


def parent(link, piece):
    dx, dy, dz = piece
    return {
        "xp": ((dx + XS - 1) % XS, dy, dz),
        "xm": ((dx + 1) % XS, dy, dz),
        "y": (dx, 1 - dy, dz),
        "zp": (dx, dy, dz - 1),
        "zm": (dx, dy, dz + 1),
    }[link]


def position():
    g = lax.axis_index("outer")
    inner = lax.axis_index("inner")
    cross_up = jnp.where(g % ZS == ZS - 1, 1, 0)
    cross_down = jnp.where(g % ZS == 0, 1, 0)
    return g, inner // (2 * XS), inner // 2 % XS, inner % 2, cross_up, cross_down


def nt_dot(a, b):
    return lax.dot_general(a, b, (((1,), (1,)), ((), ())), preferred_element_type=jnp.float32)


def query_tile(q_ref, row, t):
    rows = pl.ds(pl.multiple_of(row * BLOCK, BLOCK), BLOCK)
    return jnp.concatenate([q_ref[rows, h * HD:(h + 1) * HD] for h in (2 * t, 2 * t + 1)], axis=0)


def tiles():
    return [(t, pl.ds(t * TILE, TILE)) for t in range(HEADS * HD // TILE)]


def ahead(k, q_ref, row, scores, first=0):
    for t, c in tiles():
        scores[pl.ds(first, k.shape[0]), c] = nt_dot(k, query_tile(q_ref, row, t))


def attend_step(q_ref, scores, shift, total, acc, row, live, v, next_row, next_k, first=0):
    keys = len(live) * BLOCK
    for t, c in tiles():
        base = shift[row, 0:1, c]
        parts = []
        for e in range(len(live)):
            m = jnp.where(live[e], base, DEAD)
            parts.append(jnp.exp2(scores[pl.ds(first + e * BLOCK, BLOCK), c] * SCALE - m))
        scores[pl.ds(first, keys), c] = nt_dot(next_k, query_tile(q_ref, next_row, t))
        weights = jnp.concatenate(parts, axis=0)
        total[row, :, c] += jnp.sum(weights.reshape(keys // 8, 8, TILE), axis=0)
        acc[row, :, c] += jnp.dot(v, weights.astype(jnp.bfloat16), preferred_element_type=jnp.float32)


def sort_lists(blocks, counts, lists, pad, flat, table):
    g, y, x, _, cross_up, cross_down = position()
    pad[...] = jnp.zeros_like(pad)
    pad[0:lists, 0:MAXB] = blocks[...]
    block = pad[...]
    lane = lax.broadcasted_iota(jnp.int32, (8, LANES), 1)
    line = lax.broadcasted_iota(jnp.int32, (8, LANES), 0)
    length = jnp.zeros((8, LANES), jnp.int32)
    for row in range(lists):
        length = jnp.where(line == row, counts[row], length)
    group = (block // GROUP_BLOCKS - g + 1 + GROUPS) % GROUPS
    device = block % GROUP_BLOCKS // CH
    turn = jnp.where(group == 2, cross_up, jnp.where(group == 0, cross_down, 0))
    dx = (device // 2 % XS - x + XS) % XS
    dy = (device // (2 * XS) + y + turn) % 2
    code = group * 2 * XS + dy * XS + dx
    order = jnp.zeros_like(code)
    for i, (px, py, pz) in enumerate(ORDER):
        order = jnp.where(code == (pz + 1) * 2 * XS + py * XS + px, i, order)
    rank = (order * 2 + device % 2) * CH + block % CH

    def before(mask):
        ones = jnp.where(mask, 1, 0)
        count = ones
        for k in (1, 2, 4, 8, 16, 32):
            count = count + jnp.where(lane >= k, pltpu.roll(count, k, 1), 0)
        return count - ones

    rest = lane < length
    key = jnp.full((8, LANES), -1, jnp.int32)
    for kind, (first, end, slots) in enumerate(STAGES):
        mask = (lane < length) & (order >= first) & (order < end)
        place = before(mask)
        mask = mask & (place < slots)
        key = jnp.where(mask, kind * LANES + place, key)
        rest = rest & jnp.logical_not(mask)
    key = jnp.where(rest, len(STAGES) * LANES + before(rest), key)
    flat[...] = jnp.full((LANES, LANES), -1, jnp.int32)
    flat[0:8] = key
    keys = flat[...].T
    flat[0:8] = rank
    ranks = flat[...].T
    lane = lax.broadcasted_iota(jnp.int32, (LANES, LANES), 1)
    for row in range(lists):
        mine = jnp.broadcast_to(keys[:, row:row + 1], (LANES, LANES))
        value = jnp.broadcast_to(ranks[:, row:row + 1], (LANES, LANES)) + 1
        for kind in range(len(STAGES) + 1):
            line = jnp.sum(jnp.where(mine == kind * LANES + lane, value, 0), axis=0, keepdims=True)
            if kind == len(STAGES):
                left = jnp.sum(jnp.where(mine >= kind * LANES, 1, 0), axis=0, keepdims=True)
                line = jnp.where(lane[0:1] == LANES - 1, left, line)
            table[kind * 8 + row:kind * 8 + row + 1] = line


def gather_kernel(
    q_hbm, k_hbm, v_hbm, blocks, counts, win, acc_out, total_out, shift_out, rest_out,
    buf_a, buf_b, buf_c, buf_d, q_ref, v_ref, scores, shift, total, acc, pad, flat, table, slots,
    stage, in_sem, side_sem, out_sem, own_sem, send_sem, recv_sem, sib_send, sib_recv,
):
    g, y, x, core, cross_up, cross_down = position()
    up, down = (g + 1) % GROUPS, (g + GROUPS - 1) % GROUPS
    lists = q_ref.shape[0] // BLOCK
    buffers = (buf_a, buf_b, buf_c, buf_d)

    def place(px, py):
        return (py * XS + px) * 2 + core

    target = {
        "xp": (g, place((x + XS - 1) % XS, y)),
        "xm": (g, place((x + 1) % XS, y)),
        "y": (g, place(x, 1 - y)),
        "zp": (down, place(x, (y + cross_down) % 2)),
        "zm": (up, place(x, (y + cross_up) % 2)),
    }
    sibling = (g, (y * XS + x) * 2 + 1 - core)

    def part(order, side, c, blocks):
        for (first, end, _), buf in zip(STAGES, buffers):
            if first <= order < end:
                return buf.at[pl.ds(((order - first) * 2 + side) * CH + c, blocks)]
        return win.at[pl.ds((order * 2 + side) * CH + c, blocks)]

    def at(piece, c):
        return part(ORDER.index(piece), core, c, 1)

    def source(piece, c):
        return stage.at[pl.ds(c, 1)] if piece == ORDER[0] else at(piece, c)

    def remote(src, dst, send, recv, device):
        return pltpu.make_async_remote_copy(
            src_ref=src, dst_ref=dst, send_sem=send, recv_sem=recv, device_id=device, device_id_type=MESH
        )

    def link_copy(link, piece, c, t):
        return remote(
            source(parent(link, piece), c), at(piece, c), send_sem.at[t], recv_sem.at[t], target[link]
        )

    def sib_copy(piece, c, n, blocks):
        side = core
        order = ORDER.index(piece)
        if piece == ORDER[0]:
            src = stage.at[pl.ds(c, blocks)]
        else:
            src = part(order, side, c, blocks)
        return remote(src, part(order, side, c, blocks), sib_send.at[n], sib_recv.at[n], sibling)

    def many(blocks, sems, n):
        some = buf_a.at[pl.ds(0, blocks)]
        return remote(some, some, sems[0].at[n], sems[1].at[n], sibling)

    links, sibs = (send_sem, recv_sem), (sib_send, sib_recv)
    last_sib = 1 + 2 * len(STEPS)

    barrier = pltpu.get_barrier_semaphore()
    for device in (*target.values(), sibling):
        pl.semaphore_signal(barrier, inc=1, device_id=device, device_id_type=MESH)
    k_copies, v_copies, fill = [], [], []
    for c in range(CH):
        rows = pl.ds(c * BLOCK, BLOCK)
        k_copies.append(pltpu.make_async_copy(k_hbm.at[rows], stage.at[c, 0], in_sem.at[0, c]))
        v_copies.append(pltpu.make_async_copy(v_hbm.at[rows], v_ref.at[c], in_sem.at[1, c]))
        k_copies[c].start()
        v_copies[c].start()
    q_copy = pltpu.make_async_copy(q_hbm, q_ref, side_sem.at[0])
    q_copy.start()
    for c in range(CH):
        v_copies[c].wait()
        stage[c, 1] = v_ref[c].T
        k_copies[c].wait()
        copy = pltpu.make_async_copy(stage.at[pl.ds(c, 1)], at(ORDER[0], c), own_sem.at[c])
        copy.start()
        fill.append(copy)
    pl.semaphore_wait(barrier, len(target) + 1)

    def row(step, c):
        if step < len(STEPS):
            return [(link, STEPS[step][link], c) for link in LINKS]
        return LAST[c]

    def when(condition, run):
        if isinstance(condition, bool):
            if condition:
                run()
        else:
            pl.when(condition)(run)

    def tick(step, c):
        t = step * CH + c
        now = row(step, c) if step < len(STEPS) or c < len(LAST) else ()
        late = [step == 1 or (link == "y" and step == 2) for link, _, _ in now]
        if now and step * CH >= AHEAD:
            if step < len(STEPS) or not isinstance(t, int):
                many(len(LINKS), links, t - AHEAD).wait_send()
            else:
                many(len(row((t - AHEAD) // CH, (t - AHEAD) % CH)), links, t - AHEAD).wait_send()
        for after in (False, True):
            if after and step > 0:
                many(len(LINKS), links, t - CH).wait_recv()
            for (link, piece, chunk), tardy in zip(now, late):
                if tardy == after:
                    link_copy(link, piece, chunk, t).start()
        if step > 0:
            def forward():
                for link, piece, _ in row(step - 1, c):
                    sib_copy(piece, c - 1, 1 + 2 * (step - 1) + c // 2, 2).start()

            when(c % 2 == 1, forward)

    for c in range(CH):
        tick(0, c)
    sib_copy(ORDER[0], 0, 0, CH).start()

    sort_lists(blocks, counts, lists, pad, flat, table)
    table_copy = pltpu.make_async_copy(table, slots, side_sem.at[1])
    table_copy.start()
    total[...] = jnp.zeros_like(total)
    acc[...] = jnp.zeros_like(acc)
    q_copy.wait()

    def peaks(row, _):
        own = stage[row, 0]
        for t, c in tiles():
            s = nt_dot(own, query_tile(q_ref, row, t))
            shift[row, :, c] = jnp.broadcast_to(jnp.max(s, axis=0, keepdims=True) * SCALE, (8, TILE))
        return 0

    def early(c, _):
        tick(1, c)
        peaks(c, 0)
        return 0

    lax.fori_loop(0, CH, early, 0)
    table_copy.wait()
    for copy in fill:
        copy.wait()

    def from_sibling(step):
        if step == 0:
            many(CH, sibs, 0).wait_recv()
        for half in range(2):
            many(2 * len(LINKS), sibs, 1 + 2 * step + half).wait_recv()

    exports = []

    def export(kind):
        first, end, _ = STAGES[kind]
        blocks_in = 2 * CH * (end - first)
        copy = pltpu.make_async_copy(
            buffers[kind], win.at[pl.ds(2 * CH * first, blocks_in)], out_sem.at[kind]
        )
        copy.start()
        exports.append(copy)

    results = []

    def deliver(pairs):
        for src, dst in pairs:
            copy = pltpu.make_async_copy(src, dst, out_sem.at[len(STAGES) + len(results)])
            copy.start()
            results.append(copy)

    deliver(((shift, shift_out), (table.at[pl.ds(8 * len(STAGES), 8)], rest_out)))

    def take(kind, meanwhile, unrolled=False):
        first, _, entries = STAGES[kind]
        buf = buffers[kind]
        subs = entries // STEP

        def codes(row, sub):
            return [slots[kind * 8 + row, sub * STEP + e] for e in range(STEP)]

        def picked(code):
            return [jnp.maximum(n - 1 - 2 * CH * first, 0) for n in code]

        def keys_of(row, sub):
            return jnp.concatenate([buf[n, 0] for n in picked(codes(row, sub))], axis=0)

        ahead(keys_of(0, 0), q_ref, 0, scores)

        def one(row, _):
            meanwhile(row)
            for sub in range(subs):
                code = codes(row, sub)
                v = jnp.concatenate([buf[n, 1] for n in picked(code)], axis=1)
                if sub + 1 < subs:
                    next_row, next_sub = row, sub + 1
                else:
                    next_row, next_sub = row + 1, 0
                    next_row = min(next_row, lists - 1) if unrolled else jnp.minimum(next_row, lists - 1)
                attend_step(
                    q_ref, scores, shift, total, acc, row, [n > 0 for n in code], v,
                    next_row, keys_of(next_row, next_sub),
                )
            if kind + 1 == len(STAGES):
                deliver(((acc.at[row], acc_out.at[row]), (total.at[row], total_out.at[row])))
            return 0

        if unrolled:
            for row in range(lists):
                one(row, 0)
        else:
            lax.fori_loop(0, lists, one, 0)

    def last_arrival(c):
        many(len(LAST[c]), links, len(STEPS) * CH + c).wait_recv()
        for link, piece, chunk in LAST[c]:
            sib_copy(piece, chunk, last_sib + c, 1).start()

    for kind in range(len(STAGES)):
        from_sibling(kind)
        export(kind)
        if kind + 2 < len(STAGES):
            take(kind, lambda c, kind=kind: tick(kind + 2, c))
        elif kind + 2 == len(STAGES):
            take(kind, lambda c: tick(len(STEPS), c), True)
        else:
            take(kind, lambda c: last_arrival(c - 1) if c > 0 else None, True)
    for t in range(TICKS - AHEAD, TICKS):
        many(len(row(t // CH, t % CH)), links, t).wait_send()
    many(CH, sibs, 0).wait_send()
    for n in range(1, last_sib):
        many(2 * len(LINKS), sibs, n).wait_send()
    for c, last in enumerate(LAST):
        many(len(last), sibs, last_sib + c).wait_send()
        many(len(last), sibs, last_sib + c).wait_recv()
    for copy in exports + results:
        copy.wait()


def gather(queries, keys, values, blocks, counts):
    lists = queries.shape[0] // BLOCK
    rows = HEADS * BLOCK
    state = (
        jax.ShapeDtypeStruct((lists, HD, rows), jnp.float32),
        jax.ShapeDtypeStruct((lists, 8, rows), jnp.float32),
        jax.ShapeDtypeStruct((lists, 8, rows), jnp.float32),
    )
    vmem = pl.BlockSpec(memory_space=pltpu.VMEM)
    kinds = len(STAGES)
    return pl.pallas_call(
        gather_kernel,
        out_shape=(
            jax.ShapeDtypeStruct((len(ORDER) * 2 * CH, 2, BLOCK, HD), jnp.bfloat16),
            *state,
            jax.ShapeDtypeStruct((8, LANES), jnp.int32),
        ),
        in_specs=[
            *[pl.BlockSpec(memory_space=pl.ANY)] * 3, vmem, pl.BlockSpec(memory_space=pltpu.SMEM),
        ],
        out_specs=(pl.BlockSpec(memory_space=pl.ANY),) * 5,
        scratch_shapes=[
            *(pltpu.VMEM((2 * CH * (end - first), 2, BLOCK, HD), jnp.bfloat16) for first, end, _ in STAGES),
            pltpu.VMEM(queries.shape, queries.dtype),
            pltpu.VMEM((CH, BLOCK, HD), jnp.bfloat16),
            pltpu.VMEM((STEP * BLOCK, rows), jnp.float32),
            pltpu.VMEM((lists, 8, rows), jnp.float32),
            pltpu.VMEM((lists, 8, rows), jnp.float32),
            pltpu.VMEM((lists, HD, rows), jnp.float32),
            pltpu.VMEM((8, LANES), jnp.int32),
            pltpu.VMEM((LANES, LANES), jnp.int32),
            pltpu.VMEM((8 * (kinds + 1), LANES), jnp.int32),
            pltpu.SMEM((8 * (kinds + 1), LANES), jnp.int32),
            pltpu.VMEM((CH, 2, BLOCK, HD), jnp.bfloat16),
            pltpu.SemaphoreType.DMA((2, CH)),
            pltpu.SemaphoreType.DMA((2,)),
            pltpu.SemaphoreType.DMA((kinds + 2 + 2 * lists,)),
            pltpu.SemaphoreType.DMA((CH,)),
            pltpu.SemaphoreType.DMA((TICKS,)),
            pltpu.SemaphoreType.DMA((TICKS,)),
            pltpu.SemaphoreType.DMA((1 + 2 * len(STEPS) + len(LAST),)),
            pltpu.SemaphoreType.DMA((1 + 2 * len(STEPS) + len(LAST),)),
        ],
        compiler_params=pltpu.CompilerParams(
            collective_id=0, has_side_effects=True, vmem_limit_bytes=VMEM_LIMIT
        ),
    )(queries, keys, values, blocks, counts)


def rest_kernel(
    rest_hbm, blocks_hbm, counts_hbm, q_hbm, win, acc_hbm, total_hbm, shift_hbm, o_hbm,
    kv, q_ref, scores, shift, total, acc, out, rest, blocks, counts, places, plan, sem, side_sem, out_sem,
):
    g, y, x, _, cross_up, cross_down = position()
    lists = q_ref.shape[0] // BLOCK
    q_copy = pltpu.make_async_copy(q_hbm, q_ref, side_sem.at[0])
    shift_copy = pltpu.make_async_copy(shift_hbm, shift, side_sem.at[1])
    total_copy = pltpu.make_async_copy(total_hbm, total, side_sem.at[2])
    acc_copy = pltpu.make_async_copy(acc_hbm, acc, side_sem.at[3])

    def fetch(n, e, source):
        return pltpu.make_async_copy(win.at[source], kv.at[n, e], sem.at[n, e])

    def plan_part(n, row, codes):
        plan[n, PART] = row
        for e, code in enumerate(codes):
            plan[n, e] = code
            fetch(n, e, jnp.maximum(code - 1, 0)).start()

    def plan_list(row, n):
        def one(s, n):
            plan_part(n, row, [rest[row, s * PART + e] for e in range(PART)])
            return n + 1

        return lax.fori_loop(0, (rest[row, LANES - 1] + PART - 1) // PART, one, n)

    rest_copy = pltpu.make_async_copy(rest_hbm, rest, side_sem.at[4])
    for copy in (rest_copy, q_copy, shift_copy):
        copy.start()
    rest_copy.wait()
    parts = lax.fori_loop(0, lists, plan_list, 0)

    @pl.when(parts % 2 == 1)
    def _():
        plan_part(parts, 0, [0] * PART)

    steps = (parts + 1) // 2
    for copy in (total_copy, acc_copy):
        copy.start()

    def wait(n):
        for e in range(PART):
            fetch(2 * n, e, 0).wait()
            fetch(2 * n + 1, e, 0).wait()

    def keys_of(n):
        return jnp.concatenate([kv[n, e, 0] for e in range(PART)], axis=0)

    q_copy.wait()

    @pl.when(steps > 0)
    def _():
        wait(0)
        for n in range(2):
            ahead(keys_of(n), q_ref, plan[n, PART], scores, n * PART * BLOCK)

    for copy in (shift_copy, total_copy, acc_copy):
        copy.wait()

    def step(n, _):
        following = jnp.minimum(n + 1, steps - 1)

        @pl.when(n + 1 < steps)
        def _():
            wait(n + 1)

        for half in range(2):
            now, later = 2 * n + half, 2 * following + half
            v = jnp.concatenate([kv[now, e, 1] for e in range(PART)], axis=1)
            attend_step(
                q_ref, scores, shift, total, acc, plan[now, PART], [plan[now, e] > 0 for e in range(PART)], v,
                plan[later, PART], keys_of(later), half * PART * BLOCK,
            )
        return 0

    lax.fori_loop(0, steps, step, 0)

    def rank(block):
        group = (block // GROUP_BLOCKS - g + 1 + GROUPS) % GROUPS
        device = block % GROUP_BLOCKS // CH
        turn = jnp.where(group == 2, cross_up, jnp.where(group == 0, cross_down, 0))
        dx = (device // 2 % XS - x + XS) % XS
        dy = (device // (2 * XS) + y + turn) % 2
        return (places[group * 2 * XS + dy * XS + dx] * 2 + device % 2) * CH + block % CH

    def again(row, _):
        for t, c in tiles():
            q = query_tile(q_ref, row, t)

            def one(e, state, q=q):
                peak, tot, mixed = state
                copy = fetch(0, 0, rank(blocks[row, e]))
                copy.start()
                copy.wait()
                s = nt_dot(kv[0, 0, 0], q) * SCALE
                new = jnp.maximum(peak, jnp.max(s, axis=0, keepdims=True))
                weights = jnp.exp2(s - new)
                keep = jnp.exp2(peak - new)
                tot = tot * keep + jnp.sum(weights, axis=0, keepdims=True)
                mixed = mixed * keep + jnp.dot(
                    kv[0, 0, 1], weights.astype(jnp.bfloat16), preferred_element_type=jnp.float32
                )
                return new, tot, mixed

            start = (
                jnp.full((1, TILE), -DEAD, jnp.float32),
                jnp.zeros((1, TILE), jnp.float32),
                jnp.zeros((HD, TILE), jnp.float32),
            )
            _, tot, mixed = lax.fori_loop(0, counts[row], one, start)
            total[row, :, c] = jnp.concatenate([tot, jnp.zeros((7, TILE), jnp.float32)], axis=0)
            acc[row, :, c] = mixed
        return 0

    safe = jnp.max(jnp.sum(total[...], axis=1)) < LIMIT

    @pl.when(jnp.logical_not(safe))
    def _():
        for n, (src, dst) in enumerate(((blocks_hbm, blocks), (counts_hbm, counts))):
            copy = pltpu.make_async_copy(src, dst, side_sem.at[n])
            copy.start()
            copy.wait()
        for i, (dx, dy, dz) in enumerate(ORDER):
            places[(dz + 1) * 2 * XS + dy * XS + dx] = i
        lax.fori_loop(0, lists, again, 0)

    def finish(row, _):
        scale = 1.0 / jnp.sum(total[row], axis=0, keepdims=True)
        rows = pl.ds(pl.multiple_of(row * BLOCK, BLOCK), BLOCK)
        for h in range(HEADS):
            c = slice(h * HD, (h + 1) * HD)
            out[rows, c] = (acc[row, :, c] * scale[:, c]).astype(jnp.bfloat16).T
        pltpu.make_async_copy(out.at[rows], o_hbm.at[rows], out_sem.at[row]).start()
        return 0

    lax.fori_loop(0, lists, finish, 0)

    def sent(row, _):
        rows = pl.ds(pl.multiple_of(row * BLOCK, BLOCK), BLOCK)
        pltpu.make_async_copy(out.at[rows], o_hbm.at[rows], out_sem.at[row]).wait()
        return 0

    lax.fori_loop(0, lists, sent, 0)


def attend_rest(rest, blocks, counts, queries, window, acc, total, shift):
    lists = queries.shape[0] // BLOCK
    parts = lists * (MAXB // PART)
    rows = HEADS * BLOCK
    hbm = pl.BlockSpec(memory_space=pl.ANY)
    return pl.pallas_call(
        rest_kernel,
        in_specs=[hbm] * 8,
        out_specs=hbm,
        scratch_shapes=[
            pltpu.VMEM((parts, PART, 2, BLOCK, HD), jnp.bfloat16),
            pltpu.VMEM(queries.shape, queries.dtype),
            pltpu.VMEM((STEP * BLOCK, rows), jnp.float32),
            *[pltpu.VMEM((lists, 8, rows), jnp.float32)] * 2,
            pltpu.VMEM((lists, HD, rows), jnp.float32),
            pltpu.VMEM(queries.shape, queries.dtype),
            pltpu.SMEM(rest.shape, jnp.int32),
            pltpu.SMEM(blocks.shape, jnp.int32),
            pltpu.SMEM(counts.shape, jnp.int32),
            pltpu.SMEM((len(ORDER),), jnp.int32),
            pltpu.SMEM((parts, PART + 1), jnp.int32),
            pltpu.SemaphoreType.DMA((parts, PART)),
            pltpu.SemaphoreType.DMA((5,)),
            pltpu.SemaphoreType.DMA((lists,)),
        ],
        out_shape=jax.ShapeDtypeStruct(queries.shape, jnp.bfloat16),
        compiler_params=pltpu.CompilerParams(vmem_limit_bytes=VMEM_LIMIT),
    )(rest, blocks, counts, queries, window, acc, total, shift)


def body(queries, keys, values, key_blocks, key_counts):
    window, acc, total, shift, rest = gather(queries, keys, values, key_blocks, key_counts)
    return attend_rest(rest, key_blocks, key_counts, queries, window, acc, total, shift)


def solution(mesh):
    placed = (
        P(("outer", "inner"), None),
        P(("outer", "inner"), None),
        P(("outer", "inner"), None),
        P(("outer", "inner"), None),
        P(("outer", "inner")),
    )
    return jax.shard_map(
        body, mesh=mesh, in_specs=placed, out_specs=P(("outer", "inner"), None), check_vma=False
    )
```

```python
import functools

import jax
import jax.numpy as jnp
from jax import lax
from jax.experimental import pallas as pl
from jax.experimental.pallas import tpu as pltpu
from jax.sharding import PartitionSpec as P

HD = 128
HEADS = 8
BLOCK = 128
MAXB = 44
XS = 4
ZS = 8
CH = 4
GROUP_BLOCKS = 64
STEP = 4
PART = 2
TILE = 2 * HD
GROUPS = 16
SCALE = HD ** -0.5 * 1.4426950408889634
LIMIT = 2.0 ** 100
DEAD = 1e30
LANES = 128
VMEM_LIMIT = 60 * 2 ** 20
MESH = pl.DeviceIdType.MESH

LINKS = ("xp", "xm", "y", "zp", "zm")
STEPS = (
    {"xp": (1, 0, 0), "xm": (3, 0, 0), "y": (0, 1, 0), "zp": (0, 0, 1), "zm": (0, 0, -1)},
    {"xp": (2, 0, 0), "xm": (3, 0, 1), "y": (1, 1, 0), "zp": (1, 0, 1), "zm": (3, 0, -1)},
    {"xp": (1, 0, -1), "xm": (3, 1, 0), "y": (2, 1, 0), "zp": (0, 1, 1), "zm": (0, 1, -1)},
    {"xp": (2, 0, 1), "xm": (2, 0, -1), "y": (3, 1, 1), "zp": (1, 1, 1), "zm": (1, 1, -1)},
)
LAST = (
    (("xm", (3, 1, -1), 0, None), ("y", (3, 1, -1), 3, None), ("zm", (2, 1, -1), 3, None), ("zp", (2, 1, 1), 3, None),
     ("xp", (2, 1, 1), 0, None)),
    (("xm", (3, 1, -1), 1, None), ("y", (3, 1, -1), 2, None), ("zm", (2, 1, -1), 2, None), ("zp", (2, 1, 1), 2, None),
     ("xp", (2, 1, -1), 0, None)),
    (("xm", (2, 1, 1), 1, 1), ("xp", (2, 1, -1), 1, 1), ("zm", (2, 1, -1), 1, 0), ("zp", (2, 1, 1), 1, 0)),
)
ORDER = ((0, 0, 0),) + tuple(row[link] for row in STEPS for link in LINKS) + ((3, 1, -1), (2, 1, 1), (2, 1, -1))
STAGES = ((0, 6, 8), (6, 11, 8), (11, 16, 8), (16, 21, 4))
TICKS = CH * len(STEPS) + len(LAST)
AHEAD = 4


def parent(link, piece):
    dx, dy, dz = piece
    return {
        "xp": ((dx + XS - 1) % XS, dy, dz),
        "xm": ((dx + 1) % XS, dy, dz),
        "y": (dx, 1 - dy, dz),
        "zp": (dx, dy, dz - 1),
        "zm": (dx, dy, dz + 1),
    }[link]


def position():
    g = lax.axis_index("outer")
    inner = lax.axis_index("inner")
    cross_up = jnp.where(g % ZS == ZS - 1, 1, 0)
    cross_down = jnp.where(g % ZS == 0, 1, 0)
    return g, inner // (2 * XS), inner // 2 % XS, inner % 2, cross_up, cross_down


def nt_dot(a, b):
    return lax.dot_general(a, b, (((1,), (1,)), ((), ())), preferred_element_type=jnp.float32)


def query_tile(q_ref, row, t):
    rows = pl.ds(pl.multiple_of(row * BLOCK, BLOCK), BLOCK)
    return jnp.concatenate([q_ref[rows, h * HD:(h + 1) * HD] for h in (2 * t, 2 * t + 1)], axis=0)


def tiles():
    return [(t, pl.ds(t * TILE, TILE)) for t in range(HEADS * HD // TILE)]


def ahead(k, q_ref, row, scores, first=0):
    for t, c in tiles():
        scores[pl.ds(first, k.shape[0]), c] = nt_dot(k, query_tile(q_ref, row, t))


def attend_step(q_ref, scores, shift, total, acc, row, live, v, next_row, next_k, first=0):
    keys = len(live) * BLOCK
    for t, c in tiles():
        base = shift[row, 0:1, c]
        parts = []
        for e in range(len(live)):
            m = jnp.where(live[e], base, DEAD)
            parts.append(jnp.exp2(scores[pl.ds(first + e * BLOCK, BLOCK), c] * SCALE - m))
        scores[pl.ds(first, keys), c] = nt_dot(next_k, query_tile(q_ref, next_row, t))
        weights = jnp.concatenate(parts, axis=0)
        total[row, :, c] += jnp.sum(weights.reshape(keys // 8, 8, TILE), axis=0)
        acc[row, :, c] += jnp.dot(v, weights.astype(jnp.bfloat16), preferred_element_type=jnp.float32)


def sort_lists(blocks, counts, lists, pad, flat, table):
    g, y, x, _, cross_up, cross_down = position()
    pad[...] = jnp.zeros_like(pad)
    pad[0:lists, 0:MAXB] = blocks[...]
    block = pad[...]
    lane = lax.broadcasted_iota(jnp.int32, (8, LANES), 1)
    line = lax.broadcasted_iota(jnp.int32, (8, LANES), 0)
    length = jnp.zeros((8, LANES), jnp.int32)
    for row in range(lists):
        length = jnp.where(line == row, counts[row], length)
    group = (block // GROUP_BLOCKS - g + 1 + GROUPS) % GROUPS
    device = block % GROUP_BLOCKS // CH
    turn = jnp.where(group == 2, cross_up, jnp.where(group == 0, cross_down, 0))
    dx = (device // 2 % XS - x + XS) % XS
    dy = (device // (2 * XS) + y + turn) % 2
    code = group * 2 * XS + dy * XS + dx
    order = jnp.zeros_like(code)
    for i, (px, py, pz) in enumerate(ORDER):
        order = jnp.where(code == (pz + 1) * 2 * XS + py * XS + px, i, order)
    rank = (order * 2 + device % 2) * CH + block % CH

    def before(mask):
        ones = jnp.where(mask, 1, 0)
        count = ones
        for k in (1, 2, 4, 8, 16, 32):
            count = count + jnp.where(lane >= k, pltpu.roll(count, k, 1), 0)
        return count - ones

    rest = (lane > 0) & (lane < length)
    key = jnp.full((8, LANES), -1, jnp.int32)
    for kind, (first, end, slots) in enumerate(STAGES):
        mask = (lane > 0) & (lane < length) & (order >= first) & (order < end)
        place = before(mask)
        mask = mask & (place < slots)
        key = jnp.where(mask, kind * LANES + place, key)
        rest = rest & jnp.logical_not(mask)
    key = jnp.where(rest, len(STAGES) * LANES + before(rest), key)
    flat[...] = jnp.full((LANES, LANES), -1, jnp.int32)
    flat[0:8] = key
    keys = flat[...].T
    flat[0:8] = rank
    ranks = flat[...].T
    lane = lax.broadcasted_iota(jnp.int32, (LANES, LANES), 1)
    for row in range(lists):
        mine = jnp.broadcast_to(keys[:, row:row + 1], (LANES, LANES))
        value = jnp.broadcast_to(ranks[:, row:row + 1], (LANES, LANES)) + 1
        for kind in range(len(STAGES) + 1):
            line = jnp.sum(jnp.where(mine == kind * LANES + lane, value, 0), axis=0, keepdims=True)
            if kind == len(STAGES):
                left = jnp.sum(jnp.where(mine >= kind * LANES, 1, 0), axis=0, keepdims=True)
                line = jnp.where(lane[0:1] == LANES - 1, left, line)
            table[kind * 8 + row:kind * 8 + row + 1] = line


def gather_kernel(
    q_hbm, k_hbm, v_hbm, blocks, counts, win, acc_out, total_out, shift_out, rest_out,
    buf_a, buf_b, buf_c, buf_d, q_ref, v_ref, scores, shift, total, acc, pad, flat, table, slots,
    stage, in_sem, side_sem, out_sem, own_sem, send_sem, recv_sem, sib_send, sib_recv,
):
    g, y, x, core, cross_up, cross_down = position()
    up, down = (g + 1) % GROUPS, (g + GROUPS - 1) % GROUPS
    lists = q_ref.shape[0] // BLOCK
    buffers = (buf_a, buf_b, buf_c, buf_d)

    def place(px, py):
        return (py * XS + px) * 2 + core

    target = {
        "xp": (g, place((x + XS - 1) % XS, y)),
        "xm": (g, place((x + 1) % XS, y)),
        "y": (g, place(x, 1 - y)),
        "zp": (down, place(x, (y + cross_down) % 2)),
        "zm": (up, place(x, (y + cross_up) % 2)),
    }
    sibling = (g, (y * XS + x) * 2 + 1 - core)

    def part(order, side, c, blocks):
        for (first, end, _), buf in zip(STAGES, buffers):
            if first <= order < end:
                return buf.at[pl.ds(((order - first) * 2 + side) * CH + c, blocks)]
        return win.at[pl.ds((order * 2 + side) * CH + c, blocks)]

    def at(piece, c, half=None):
        chunk = part(ORDER.index(piece), core, c, 1)
        return chunk if half is None else chunk.at[0, half]

    def source(piece, c, half=None):
        return stage.at[pl.ds(c, 1)] if piece == ORDER[0] else at(piece, c, half)

    def remote(src, dst, send, recv, device):
        return pltpu.make_async_remote_copy(
            src_ref=src, dst_ref=dst, send_sem=send, recv_sem=recv, device_id=device, device_id_type=MESH
        )

    def link_copy(link, piece, c, half, t):
        return remote(
            source(parent(link, piece), c, half), at(piece, c, half), send_sem.at[t], recv_sem.at[t], target[link]
        )

    def chunks(items):
        return sum(2 if half is None else 1 for _, _, _, half in items) // 2

    def sib_copy(piece, c, n, blocks):
        side = core
        order = ORDER.index(piece)
        if piece == ORDER[0]:
            src = stage.at[pl.ds(c, blocks)]
        else:
            src = part(order, side, c, blocks)
        return remote(src, part(order, side, c, blocks), sib_send.at[n], sib_recv.at[n], sibling)

    def many(blocks, sems, n):
        some = buf_a.at[pl.ds(0, blocks)]
        return remote(some, some, sems[0].at[n], sems[1].at[n], sibling)

    links, sibs = (send_sem, recv_sem), (sib_send, sib_recv)
    last_sib = 1 + 2 * len(STEPS)

    barrier = pltpu.get_barrier_semaphore()
    for device in (*target.values(), sibling):
        pl.semaphore_signal(barrier, inc=1, device_id=device, device_id_type=MESH)
    k_copies, v_copies, fill = [], [], []
    for c in range(CH):
        rows = pl.ds(c * BLOCK, BLOCK)
        k_copies.append(pltpu.make_async_copy(k_hbm.at[rows], stage.at[c, 0], in_sem.at[0, c]))
        v_copies.append(pltpu.make_async_copy(v_hbm.at[rows], v_ref.at[c], in_sem.at[1, c]))
        k_copies[c].start()
        v_copies[c].start()
    q_copy = pltpu.make_async_copy(q_hbm, q_ref, side_sem.at[0])
    q_copy.start()

    def ready(c):
        v_copies[c].wait()
        stage[c, 1] = v_ref[c].T
        k_copies[c].wait()

    ready(0)
    pl.semaphore_wait(barrier, len(target) + 1)

    def row(step, c):
        if step < len(STEPS):
            return [(link, STEPS[step][link], c, None) for link in LINKS]
        return LAST[c]

    def when(condition, run):
        if isinstance(condition, bool):
            if condition:
                run()
        else:
            pl.when(condition)(run)

    def tick(step, c):
        t = step * CH + c
        now = row(step, c) if step < len(STEPS) or c < len(LAST) else ()
        late = [
            step == 1 or (step, link) == (2, "y") or (step == len(STEPS) and (c, link) == (0, "xp"))
            for link, _, _, _ in now
        ]
        if now and step * CH >= AHEAD:
            if step < len(STEPS) or not isinstance(t, int):
                many(len(LINKS), links, t - AHEAD).wait_send()
            else:
                many(chunks(row((t - AHEAD) // CH, (t - AHEAD) % CH)), links, t - AHEAD).wait_send()
        for after in (False, True):
            if after and step > 0:
                many(len(LINKS), links, t - CH).wait_recv()
            for item, tardy in zip(now, late):
                if tardy == after:
                    link_copy(*item, t).start()
        if step > 0:
            def forward():
                for _, piece, _, _ in row(step - 1, c):
                    sib_copy(piece, c - 1, 1 + 2 * (step - 1) + c // 2, 2).start()

            when(c % 2 == 1, forward)

    for c in range(CH):
        if c > 0:
            ready(c)
        tick(0, c)
    sib_copy(ORDER[0], 0, 0, CH).start()
    for c in range(CH):
        copy = pltpu.make_async_copy(stage.at[pl.ds(c, 1)], at(ORDER[0], c), own_sem.at[c])
        copy.start()
        fill.append(copy)

    sort_lists(blocks, counts, lists, pad, flat, table)
    table_copy = pltpu.make_async_copy(table, slots, side_sem.at[1])
    table_copy.start()
    q_copy.wait()

    def attend_own(row):
        for t, c in tiles():
            s = nt_dot(stage[row, 0], query_tile(q_ref, row, t)) * SCALE
            peak = jnp.max(s, axis=0, keepdims=True)
            shift[row, :, c] = jnp.broadcast_to(peak, (8, TILE))
            weights = jnp.exp2(s - peak)
            total[row, :, c] = jnp.sum(weights.reshape(BLOCK // 8, 8, TILE), axis=0)
            acc[row, :, c] = jnp.dot(
                stage[row, 1], weights.astype(jnp.bfloat16), preferred_element_type=jnp.float32
            )

    def early(c, _):
        tick(1, c)
        attend_own(c)
        return 0

    lax.fori_loop(0, CH, early, 0)
    table_copy.wait()
    for copy in fill:
        copy.wait()

    def from_sibling(step):
        if step == 0:
            many(CH, sibs, 0).wait_recv()
        for half in range(2):
            many(2 * len(LINKS), sibs, 1 + 2 * step + half).wait_recv()

    exports = []

    def export(kind):
        first, end, _ = STAGES[kind]
        blocks_in = 2 * CH * (end - first)
        copy = pltpu.make_async_copy(
            buffers[kind], win.at[pl.ds(2 * CH * first, blocks_in)], out_sem.at[kind]
        )
        copy.start()
        exports.append(copy)

    results = []

    def deliver(pairs):
        for src, dst in pairs:
            copy = pltpu.make_async_copy(src, dst, out_sem.at[len(STAGES) + len(results)])
            copy.start()
            results.append(copy)

    deliver(((shift, shift_out), (table.at[pl.ds(8 * len(STAGES), 8)], rest_out)))

    def take(kind, meanwhile, unrolled=False):
        first, _, entries = STAGES[kind]
        buf = buffers[kind]
        subs = entries // STEP

        def codes(row, sub):
            return [slots[kind * 8 + row, sub * STEP + e] for e in range(STEP)]

        def picked(code):
            return [jnp.maximum(n - 1 - 2 * CH * first, 0) for n in code]

        def keys_of(row, sub):
            return jnp.concatenate([buf[n, 0] for n in picked(codes(row, sub))], axis=0)

        ahead(keys_of(0, 0), q_ref, 0, scores)

        def one(row, _):
            meanwhile(row)
            for sub in range(subs):
                code = codes(row, sub)
                v = jnp.concatenate([buf[n, 1] for n in picked(code)], axis=1)
                if sub + 1 < subs:
                    next_row, next_sub = row, sub + 1
                else:
                    next_row, next_sub = row + 1, 0
                    next_row = min(next_row, lists - 1) if unrolled else jnp.minimum(next_row, lists - 1)
                attend_step(
                    q_ref, scores, shift, total, acc, row, [n > 0 for n in code], v,
                    next_row, keys_of(next_row, next_sub),
                )
            if kind + 1 == len(STAGES):
                deliver(((acc.at[row], acc_out.at[row]), (total.at[row], total_out.at[row])))
            return 0

        if unrolled:
            for row in range(lists):
                one(row, 0)
        else:
            lax.fori_loop(0, lists, one, 0)

    def last_arrival(c):
        many(chunks(LAST[c]), links, len(STEPS) * CH + c).wait_recv()
        for _, piece, chunk, half in LAST[c]:
            ref = at(piece, chunk, half)
            remote(ref, ref, sib_send.at[last_sib + c], sib_recv.at[last_sib + c], sibling).start()

    for kind in range(len(STAGES)):
        from_sibling(kind)
        export(kind)
        if kind + 2 < len(STAGES):
            take(kind, lambda c, kind=kind: tick(kind + 2, c))
        elif kind + 2 == len(STAGES):
            take(kind, lambda c: tick(len(STEPS), c), True)
        else:
            take(kind, lambda c: last_arrival(c - 1) if c > 0 else None, True)
    for t in range(TICKS - AHEAD, TICKS):
        many(chunks(row(t // CH, t % CH)), links, t).wait_send()
    many(CH, sibs, 0).wait_send()
    for n in range(1, last_sib):
        many(2 * len(LINKS), sibs, n).wait_send()
    for c, last in enumerate(LAST):
        many(chunks(last), sibs, last_sib + c).wait_send()
        many(chunks(last), sibs, last_sib + c).wait_recv()
    for copy in exports + results:
        copy.wait()


def gather(queries, keys, values, blocks, counts):
    lists = queries.shape[0] // BLOCK
    rows = HEADS * BLOCK
    state = (
        jax.ShapeDtypeStruct((lists, HD, rows), jnp.float32),
        jax.ShapeDtypeStruct((lists, 8, rows), jnp.float32),
        jax.ShapeDtypeStruct((lists, 8, rows), jnp.float32),
    )
    vmem = pl.BlockSpec(memory_space=pltpu.VMEM)
    kinds = len(STAGES)
    return pl.pallas_call(
        gather_kernel,
        out_shape=(
            jax.ShapeDtypeStruct((len(ORDER) * 2 * CH, 2, BLOCK, HD), jnp.bfloat16),
            *state,
            jax.ShapeDtypeStruct((8, LANES), jnp.int32),
        ),
        in_specs=[
            *[pl.BlockSpec(memory_space=pl.ANY)] * 3, vmem, pl.BlockSpec(memory_space=pltpu.SMEM),
        ],
        out_specs=(pl.BlockSpec(memory_space=pl.ANY),) * 5,
        scratch_shapes=[
            *(pltpu.VMEM((2 * CH * (end - first), 2, BLOCK, HD), jnp.bfloat16) for first, end, _ in STAGES),
            pltpu.VMEM(queries.shape, queries.dtype),
            pltpu.VMEM((CH, BLOCK, HD), jnp.bfloat16),
            pltpu.VMEM((STEP * BLOCK, rows), jnp.float32),
            pltpu.VMEM((lists, 8, rows), jnp.float32),
            pltpu.VMEM((lists, 8, rows), jnp.float32),
            pltpu.VMEM((lists, HD, rows), jnp.float32),
            pltpu.VMEM((8, LANES), jnp.int32),
            pltpu.VMEM((LANES, LANES), jnp.int32),
            pltpu.VMEM((8 * (kinds + 1), LANES), jnp.int32),
            pltpu.SMEM((8 * (kinds + 1), LANES), jnp.int32),
            pltpu.VMEM((CH, 2, BLOCK, HD), jnp.bfloat16),
            pltpu.SemaphoreType.DMA((2, CH)),
            pltpu.SemaphoreType.DMA((2,)),
            pltpu.SemaphoreType.DMA((kinds + 2 + 2 * lists,)),
            pltpu.SemaphoreType.DMA((CH,)),
            pltpu.SemaphoreType.DMA((TICKS,)),
            pltpu.SemaphoreType.DMA((TICKS,)),
            pltpu.SemaphoreType.DMA((1 + 2 * len(STEPS) + len(LAST),)),
            pltpu.SemaphoreType.DMA((1 + 2 * len(STEPS) + len(LAST),)),
        ],
        compiler_params=pltpu.CompilerParams(
            collective_id=0, has_side_effects=True, vmem_limit_bytes=VMEM_LIMIT
        ),
    )(queries, keys, values, blocks, counts)


def rest_kernel(
    rest_hbm, blocks_hbm, counts_hbm, q_hbm, win, acc_hbm, total_hbm, shift_hbm, o_hbm,
    kv, q_ref, scores, shift, total, acc, out, rest, blocks, counts, places, plan, sem, side_sem, out_sem,
):
    g, y, x, _, cross_up, cross_down = position()
    lists = q_ref.shape[0] // BLOCK
    q_copy = pltpu.make_async_copy(q_hbm, q_ref, side_sem.at[0])
    shift_copy = pltpu.make_async_copy(shift_hbm, shift, side_sem.at[1])
    total_copy = pltpu.make_async_copy(total_hbm, total, side_sem.at[2])
    acc_copy = pltpu.make_async_copy(acc_hbm, acc, side_sem.at[3])

    def fetch(n, e, source):
        return pltpu.make_async_copy(win.at[source], kv.at[n, e], sem.at[n, e])

    def plan_part(n, row, codes):
        plan[n, PART] = row
        for e, code in enumerate(codes):
            plan[n, e] = code
            fetch(n, e, jnp.maximum(code - 1, 0)).start()

    def plan_list(row, n):
        def one(s, n):
            plan_part(n, row, [rest[row, s * PART + e] for e in range(PART)])
            return n + 1

        return lax.fori_loop(0, (rest[row, LANES - 1] + PART - 1) // PART, one, n)

    rest_copy = pltpu.make_async_copy(rest_hbm, rest, side_sem.at[4])
    for copy in (rest_copy, q_copy, shift_copy, total_copy, acc_copy):
        copy.start()
    rest_copy.wait()
    parts = lax.fori_loop(0, lists, plan_list, 0)

    @pl.when(parts % 2 == 1)
    def _():
        plan_part(parts, 0, [0] * PART)

    steps = (parts + 1) // 2

    def wait(n):
        for e in range(PART):
            fetch(2 * n, e, 0).wait()
            fetch(2 * n + 1, e, 0).wait()

    def keys_of(n):
        return jnp.concatenate([kv[n, e, 0] for e in range(PART)], axis=0)

    q_copy.wait()

    @pl.when(steps > 0)
    def _():
        wait(0)
        for n in range(2):
            ahead(keys_of(n), q_ref, plan[n, PART], scores, n * PART * BLOCK)

    for copy in (shift_copy, total_copy, acc_copy):
        copy.wait()

    def step(n, _):
        following = jnp.minimum(n + 1, steps - 1)

        @pl.when(n + 1 < steps)
        def _():
            wait(n + 1)

        for half in range(2):
            now, later = 2 * n + half, 2 * following + half
            v = jnp.concatenate([kv[now, e, 1] for e in range(PART)], axis=1)
            attend_step(
                q_ref, scores, shift, total, acc, plan[now, PART], [plan[now, e] > 0 for e in range(PART)], v,
                plan[later, PART], keys_of(later), half * PART * BLOCK,
            )
        return 0

    lax.fori_loop(0, steps, step, 0)

    def rank(block):
        group = (block // GROUP_BLOCKS - g + 1 + GROUPS) % GROUPS
        device = block % GROUP_BLOCKS // CH
        turn = jnp.where(group == 2, cross_up, jnp.where(group == 0, cross_down, 0))
        dx = (device // 2 % XS - x + XS) % XS
        dy = (device // (2 * XS) + y + turn) % 2
        return (places[group * 2 * XS + dy * XS + dx] * 2 + device % 2) * CH + block % CH

    def again(row, _):
        for t, c in tiles():
            q = query_tile(q_ref, row, t)

            def one(e, state, q=q):
                peak, tot, mixed = state
                copy = fetch(0, 0, rank(blocks[row, e]))
                copy.start()
                copy.wait()
                s = nt_dot(kv[0, 0, 0], q) * SCALE
                new = jnp.maximum(peak, jnp.max(s, axis=0, keepdims=True))
                weights = jnp.exp2(s - new)
                keep = jnp.exp2(peak - new)
                tot = tot * keep + jnp.sum(weights, axis=0, keepdims=True)
                mixed = mixed * keep + jnp.dot(
                    kv[0, 0, 1], weights.astype(jnp.bfloat16), preferred_element_type=jnp.float32
                )
                return new, tot, mixed

            start = (
                jnp.full((1, TILE), -DEAD, jnp.float32),
                jnp.zeros((1, TILE), jnp.float32),
                jnp.zeros((HD, TILE), jnp.float32),
            )
            _, tot, mixed = lax.fori_loop(0, counts[row], one, start)
            total[row, :, c] = jnp.concatenate([tot, jnp.zeros((7, TILE), jnp.float32)], axis=0)
            acc[row, :, c] = mixed
        return 0

    safe = jnp.max(jnp.sum(total[...], axis=1)) < LIMIT

    @pl.when(jnp.logical_not(safe))
    def _():
        for n, (src, dst) in enumerate(((blocks_hbm, blocks), (counts_hbm, counts))):
            copy = pltpu.make_async_copy(src, dst, side_sem.at[n])
            copy.start()
            copy.wait()
        for i, (dx, dy, dz) in enumerate(ORDER):
            places[(dz + 1) * 2 * XS + dy * XS + dx] = i
        lax.fori_loop(0, lists, again, 0)

    def finish(row, _):
        scale = 1.0 / jnp.sum(total[row], axis=0, keepdims=True)
        rows = pl.ds(pl.multiple_of(row * BLOCK, BLOCK), BLOCK)
        for h in range(HEADS):
            c = slice(h * HD, (h + 1) * HD)
            out[rows, c] = (acc[row, :, c] * scale[:, c]).astype(jnp.bfloat16).T
        pltpu.make_async_copy(out.at[rows], o_hbm.at[rows], out_sem.at[row]).start()
        return 0

    lax.fori_loop(0, lists, finish, 0)

    def sent(row, _):
        rows = pl.ds(pl.multiple_of(row * BLOCK, BLOCK), BLOCK)
        pltpu.make_async_copy(out.at[rows], o_hbm.at[rows], out_sem.at[row]).wait()
        return 0

    lax.fori_loop(0, lists, sent, 0)


def attend_rest(rest, blocks, counts, queries, window, acc, total, shift):
    lists = queries.shape[0] // BLOCK
    parts = lists * (MAXB // PART)
    rows = HEADS * BLOCK
    hbm = pl.BlockSpec(memory_space=pl.ANY)
    return pl.pallas_call(
        rest_kernel,
        in_specs=[hbm] * 8,
        out_specs=hbm,
        scratch_shapes=[
            pltpu.VMEM((parts, PART, 2, BLOCK, HD), jnp.bfloat16),
            pltpu.VMEM(queries.shape, queries.dtype),
            pltpu.VMEM((STEP * BLOCK, rows), jnp.float32),
            *[pltpu.VMEM((lists, 8, rows), jnp.float32)] * 2,
            pltpu.VMEM((lists, HD, rows), jnp.float32),
            pltpu.VMEM(queries.shape, queries.dtype),
            pltpu.SMEM(rest.shape, jnp.int32),
            pltpu.SMEM(blocks.shape, jnp.int32),
            pltpu.SMEM(counts.shape, jnp.int32),
            pltpu.SMEM((len(ORDER),), jnp.int32),
            pltpu.SMEM((parts, PART + 1), jnp.int32),
            pltpu.SemaphoreType.DMA((parts, PART)),
            pltpu.SemaphoreType.DMA((5,)),
            pltpu.SemaphoreType.DMA((lists,)),
        ],
        out_shape=jax.ShapeDtypeStruct(queries.shape, jnp.bfloat16),
        compiler_params=pltpu.CompilerParams(vmem_limit_bytes=VMEM_LIMIT),
    )(rest, blocks, counts, queries, window, acc, total, shift)


def body(queries, keys, values, key_blocks, key_counts):
    window, acc, total, shift, rest = gather(queries, keys, values, key_blocks, key_counts)
    return attend_rest(rest, key_blocks, key_counts, queries, window, acc, total, shift)


def solution(mesh):
    placed = (
        P(("outer", "inner"), None),
        P(("outer", "inner"), None),
        P(("outer", "inner"), None),
        P(("outer", "inner"), None),
        P(("outer", "inner")),
    )
    return jax.shard_map(
        body, mesh=mesh, in_specs=placed, out_specs=P(("outer", "inner"), None), check_vma=False
    )
```
